256 devices in a mesh: lead: 16 (over y_lo, z), mesh: 16 (over x, y_hi, core).
Axes of the slice: x: 4, y: 4 (y_hi: 2, y_lo: 2; y = y_hi * 2 + y_lo), z: 8, core: 2. Of those that a mesh axis runs over, the one named last changes fastest.
Arguments:
- states: bfloat16 [16, 2, 2048, 1024], P('lead', None, 'mesh'), may hold values from -6 to 6
- entering: bfloat16 [2, 2, 2048, 1024], P(None, None, 'mesh'), may hold values from -6 to 6
- norm_gain: float32 [1024], replicated, may hold values from 0.1 to 1.9
- query_weight: bfloat16 [1024, 1024], replicated
- key_weight: bfloat16 [1024, 1024], replicated, as said below
- value_weight: bfloat16 [1024, 1024], replicated, may hold values from -0.1875 to 0.1875
- out_weight: bfloat16 [1024, 1024], replicated, may hold values from -0.1875 to 0.1875
- senders: int32 [2048, 8], P('mesh'), may hold values from 0 to 191, as said below
- halo_rows: int32 [16, 2, 32], P('mesh'), may hold values from 0 to 127
Outputs:
- advanced: bfloat16 [16, 2, 2048, 1024], P('lead', None, 'mesh')
The draws below stay inside these ranges and needn't reach their ends.
Inputs may be any that keep to these rules, and one draw needn't show every extreme that they name: senders[n, 0] is n's own position in its partition; the others index the 128 own nodes, the 32 nodes from the partition before and the 32 from the one after, in that order; the first partition names none from before and the last none from after. `key_weight`: weights of fan-in 1024.
All inputs are finite; a program needn't handle non-finite values.
Results may differ from the reference program's by a relative error of at most 0.014.
Values may be sent and summed in bfloat16 or wider, within the bound.
No kernel may reach another device: no remote copies, remote signals or barrier semaphores. Data moves between devices by JAX's collectives and lax.ppermute only.
A program may use at most 64 MiB of HBM per device.

```python
import math
import jax
import jax.numpy as jnp
from jax import lax

D = 1024
HEADS = 16
HEAD_DIM = 64
DEG = 8
NODE_DEV = 128
HALO = 32
MEMBERS = 2
TICKS = 2
LEADS = 16
PARTS_SIZE = 16
NODES = 2048
N_MESH = 16


def key_base(key):
    return jax.random.normal(key, (D, D), jnp.float32) / math.sqrt(D)


def draw_key_weight(key, part):
    shared = key_base(key)
    return shared.astype(jnp.bfloat16)


def draw_query_weight(key, part):
    key = jax.random.fold_in(key, 13)
    own = jax.random.normal(key, (D, D), jnp.float32) / math.sqrt(D)
    return own.astype(jnp.bfloat16)


def draw_senders(key, part):
    key = jax.random.fold_in(key, 17)
    node_ids = jnp.arange(NODES, dtype=jnp.int32)
    local = node_ids % NODE_DEV
    owner = node_ids // NODE_DEV
    picks = jax.random.randint(key, (NODES, DEG - 1), 0, NODE_DEV + 2 * HALO, dtype=jnp.int32)
    before = (picks >= NODE_DEV) & (picks < NODE_DEV + HALO) & (owner[:, None] == 0)
    picks = jnp.where(before, picks - NODE_DEV, picks)
    after = (picks >= NODE_DEV + HALO) & (owner[:, None] == PARTS_SIZE - 1)
    picks = jnp.where(after, picks - NODE_DEV - HALO, picks)
    topmost = (local == 0) & (owner < PARTS_SIZE - 1)
    first_pick = jnp.where(topmost, NODE_DEV + 2 * HALO - 1, picks[:, 0])
    picks = picks.at[:, 0].set(first_pick)
    return jnp.concatenate([local[:, None], picks], axis=1).astype(jnp.int32)


def touch_ends(values, rng, smallest, largest):
    longest = values.shape.index(max(values.shape))
    spots = []
    for shift in (0, 1):
        where = [jax.random.randint(jax.random.fold_in(rng, axis), (), 0, length) for axis, length in enumerate(values.shape)]
        where[longest] = (where[longest] + shift) % values.shape[longest]
        spots.append(tuple(where))
    return values.at[spots[0]].set(smallest).at[spots[1]].set(largest)


def levels(own_key, dims, cuts, least, high):
    factor_of = 1.0
    for axis_at, blocks in cuts:
        heights = jax.random.uniform(jax.random.fold_in(jax.random.fold_in(own_key, 6), axis_at), (blocks,), jnp.float32, least / len(cuts), high / len(cuts))
        factor_of = factor_of * jnp.repeat(jnp.exp(heights), dims[axis_at] // blocks).reshape((-1,) + (1,) * (len(dims) - 1 - axis_at))
    return factor_of


def noise(rng, shape, width, reach, split=(), kind=jnp.bfloat16):
    level = levels(rng, shape, split, -0.22, 0.18) if split else 1.0
    drawn = jax.random.normal(rng, shape, jnp.float32) * width * level
    return jnp.minimum(jnp.maximum(drawn, -reach), reach).astype(kind)


def setup_inputs(seed: int = 0) -> dict:
    key_list = jax.random.split(jax.random.key(seed), 10)
    states = noise(key_list[0], (LEADS, MEMBERS, NODES, D), 1.0, 6.0, ((0, 16), (2, 16)))
    entering = noise(key_list[1], (TICKS, MEMBERS, NODES, D), 1.0, 6.0, ((2, 16),))
    norm_gain = jnp.clip(1.0 + 0.18 * jax.random.normal(key_list[2], (D,), jnp.float32), 0.1, 1.9)
    query_weight = draw_query_weight(jax.random.fold_in(key_list[9], 71), 0)
    key_weight = draw_key_weight(jax.random.fold_in(key_list[9], 71), 0)
    value_weight = noise(key_list[5], (D, D), D ** -0.5, 0.1875)
    out_weight = noise(key_list[6], (D, D), D ** -0.5, 0.1875)
    senders = draw_senders(jax.random.fold_in(key_list[9], 71), 0)
    halo_rows = touch_ends(jax.random.randint(key_list[8], (PARTS_SIZE, 2, HALO), 0, NODE_DEV), jax.random.fold_in(key_list[8], 1), 0, NODE_DEV - 1).astype(jnp.int32)
    return {"states": states, "entering": entering, "norm_gain": norm_gain, "query_weight": query_weight, "key_weight": key_weight, "value_weight": value_weight, "out_weight": out_weight, "senders": senders, "halo_rows": halo_rows}


def layer_norm(state, norm_gain):
    values = state.astype(jnp.float32)
    average = lax.optimization_barrier(jnp.mean(values, axis=-1, keepdims=True))
    centred = values - average
    spread = lax.optimization_barrier(jnp.mean(centred * centred, axis=-1, keepdims=True))
    return (centred * lax.rsqrt(spread + 1e-05) * norm_gain).astype(jnp.bfloat16)

def take_rows(table, indices):
    return table[indices]

def processor(state, norm_gain, query_weight, key_weight, value_weight, out_weight, senders, halo_rows):
    normed = layer_norm(state, norm_gain)
    queries = jnp.dot(normed, query_weight, preferred_element_type=jnp.float32).astype(jnp.bfloat16)
    keys = jnp.dot(normed, key_weight, preferred_element_type=jnp.float32).astype(jnp.bfloat16)
    values = jnp.dot(normed, value_weight, preferred_element_type=jnp.float32).astype(jnp.bfloat16)
    key_value = jnp.concatenate([keys, values], axis=-1).reshape(N_MESH, NODE_DEV, 2 * D)
    outgoing = jax.vmap(take_rows)(key_value, halo_rows)
    empty_rim = jnp.zeros((1, HALO, 2 * D), jnp.bfloat16)
    from_before = jnp.concatenate([empty_rim, outgoing[:-1, 1]], axis=0)
    from_after = jnp.concatenate([outgoing[1:, 0], empty_rim], axis=0)
    extended = jnp.concatenate([key_value, from_before, from_after], axis=1)
    gathered = jax.vmap(take_rows)(extended, senders.reshape(N_MESH, NODE_DEV, DEG))
    sender_keys = gathered[..., :D].reshape(N_MESH, NODE_DEV, DEG, HEADS, HEAD_DIM).astype(jnp.float32)
    sender_values = gathered[..., D:].reshape(N_MESH, NODE_DEV, DEG, HEADS, HEAD_DIM).astype(jnp.float32)
    head_queries = queries.reshape(N_MESH, NODE_DEV, HEADS, HEAD_DIM).astype(jnp.float32)
    scores = jnp.einsum('pnhd,pnjhd->pnjh', head_queries, sender_keys) / math.sqrt(HEAD_DIM)
    scores = scores - lax.optimization_barrier(jnp.max(scores, axis=2, keepdims=True))
    expo = jnp.exp(scores)
    weights = (expo / lax.optimization_barrier(jnp.sum(expo, axis=2, keepdims=True))).astype(jnp.bfloat16)
    attended = jnp.einsum('pnjh,pnjhd->pnhd', weights.astype(jnp.float32), sender_values)
    attended = attended.reshape(NODES, D).astype(jnp.bfloat16)
    update = jnp.dot(attended, out_weight, preferred_element_type=jnp.float32)
    return (state.astype(jnp.float32) + update).astype(jnp.bfloat16)

def reference(states, entering, norm_gain, query_weight, key_weight, value_weight, out_weight, senders, halo_rows):

    def one_state(state):
        return processor(state, norm_gain, query_weight, key_weight, value_weight, out_weight, senders, halo_rows)

    def one_lead(members):
        return lax.map(one_state, members)
    current = states
    for tick_index in range(TICKS):
        moved = jnp.concatenate([entering[tick_index][None], current[:-1]], axis=0)
        current = lax.map(one_lead, moved)
    return current
```

```python
import functools
import jax
import jax.numpy as jnp
from jax import lax
from jax.experimental import pallas as pl
from jax.experimental.pallas import tpu as pltpu

HEAD_DIM = 64
LANES = 128
NEVER = -1e30
BF = jnp.bfloat16
F32 = jnp.float32
VMEM_BYTES = 24 * 1024 * 1024


def normalised(x, gain):
    values = x.astype(F32)
    centred = values - jnp.mean(values, axis=-1, keepdims=True)
    spread = jnp.mean(centred * centred, axis=-1, keepdims=True)
    return (centred * lax.rsqrt(spread + 1e-05) * gain).astype(BF)


def rows_of(table, indices):
    spots = lax.broadcasted_iota(jnp.int32, (table.shape[0], indices.shape[1]), 0)
    picks = jnp.where(spots == indices, 1.0, 0.0)
    return jnp.dot(picks.T.astype(BF), table, preferred_element_type=F32).astype(BF)


def prep_body(flag, x, other, gain, halo, senders, state, normed, low, high, table):
    chosen = jnp.where(flag[0] == 1, other[...], x[...])
    state[...] = chosen
    rows = normalised(chosen, gain[...])
    normed[...] = rows
    low[...] = rows_of(rows, halo[0:1])
    high[...] = rows_of(rows, halo[1:2])
    if table is not None:
        count = jnp.zeros(table.shape, F32)
        spots = lax.broadcasted_iota(jnp.int32, table.shape, 1)
        for j in range(senders.shape[1]):
            count += jnp.where(spots == senders[:, j:j + 1], 1.0, 0.0)
        table[...] = jnp.where(count > 0, jnp.log(count), NEVER)


def project_body(normed, wq, wk, wv, q, k, v):
    rows = normed[...]
    q[...] = (jnp.dot(rows, wq[...], preferred_element_type=F32)).astype(BF) * BF(HEAD_DIM ** -0.5)
    k[...] = jnp.dot(rows, wk[...], preferred_element_type=F32).astype(BF)
    v[...] = jnp.dot(rows, wv[...], preferred_element_type=F32).astype(BF)


def attend(state, q, k, v, before, after, table, wk, wv, wo, attended):
    halo = jnp.concatenate([before[...], after[...]], axis=0)
    more_k = jnp.dot(halo, wk[...], preferred_element_type=F32).astype(BF)
    more_v = jnp.dot(halo, wv[...], preferred_element_type=F32).astype(BF)
    bias = table[...]
    nodes, width = q.shape
    bias = jnp.concatenate([bias, bias], axis=0)
    first = lax.broadcasted_iota(jnp.int32, (nodes, LANES), 1) < HEAD_DIM
    ones = jnp.ones((table.shape[1], LANES), BF)
    for i in range(width // LANES):
        at = slice(i * LANES, (i + 1) * LANES)
        pair = q[:, at]
        zero = jnp.zeros_like(pair)
        both = jnp.concatenate([jnp.where(first, pair, zero), jnp.where(first, zero, pair)], axis=0)
        keys = jnp.concatenate([k[:, at], more_k[:, at]], axis=0)
        values = jnp.concatenate([v[:, at], more_v[:, at]], axis=0)
        scores = lax.dot_general(both, keys, (((1,), (1,)), ((), ())), preferred_element_type=F32) + bias
        expo = jnp.exp(scores - jnp.max(scores, axis=1, keepdims=True)).astype(BF)
        sums = jnp.dot(expo, jnp.concatenate([values, ones], axis=1), preferred_element_type=F32)
        top = sums[:nodes, :LANES] / sums[:nodes, LANES:]
        low = sums[nodes:, :LANES] / sums[nodes:, LANES:]
        attended[:, at] = jnp.where(first, top, low).astype(BF)
    update = jnp.dot(attended[...], wo[...], preferred_element_type=F32)
    return (state[...].astype(F32) + update).astype(BF)


def middle_body(flag, state, q, k, v, before, after, table, wk, wv, wo, other, gain, halo,
                new_state, normed, low, high, attended):
    moved = attend(state, q, k, v, before, after, table, wk, wv, wo, attended)
    chosen = jnp.where(flag[0] == 1, other[...], moved)
    new_state[...] = chosen
    rows = normalised(chosen, gain[...])
    normed[...] = rows
    low[...] = rows_of(rows, halo[0:1])
    high[...] = rows_of(rows, halo[1:2])


def last_body(state, q, k, v, before, after, table, wk, wv, wo, out, attended):
    out[...] = attend(state, q, k, v, before, after, table, wk, wv, wo, attended)

SMEM = pl.BlockSpec(memory_space=pltpu.SMEM)
VM = pl.BlockSpec(memory_space=pltpu.VMEM)

def shape(*dims, dtype=BF):
    return jax.ShapeDtypeStruct(dims, dtype)

def params():
    return pltpu.CompilerParams(vmem_limit_bytes=VMEM_BYTES)

def cost(flops, nbytes):
    return pl.CostEstimate(flops=flops, bytes_accessed=nbytes, transcendentals=0)

def prep(flag, x, other, gain, halo, senders=None):
    n, d = x.shape
    h = halo.shape[1]
    outs = [shape(n, d), shape(n, d), shape(h, d), shape(h, d)]
    ins = [flag, x, other, gain, halo]
    specs = [SMEM] + [VM] * 4
    if senders is not None:
        outs.append(shape(n, n + 2 * h, dtype=F32)); ins.append(senders); specs.append(VM)
        body = prep_body
    else:
        def body(flag, x, other, gain, halo, *outs):
            prep_body(flag, x, other, gain, halo, None, *outs, None)
    return pl.pallas_call(body, out_shape=outs, in_specs=specs, out_specs=[VM] * len(outs),
        compiler_params=params(), cost_estimate=cost(64 * n * d * 2, 8 * n * d), name="prep")(*ins)

def project(normed, wq, wk, wv):
    n, d = normed.shape
    return pl.pallas_call(project_body, out_shape=[shape(n, d)] * 3, in_specs=[VM] * 4, out_specs=[VM] * 3,
        compiler_params=params(), cost_estimate=cost(6 * n * d * d, 8 * n * d), name="project")(normed, wq, wk, wv)

def middle(flag, state, q, k, v, before, after, table, wk, wv, wo, other, gain, halo):
    n, d = state.shape
    h = halo.shape[1]
    return pl.pallas_call(middle_body, out_shape=[shape(n, d), shape(n, d), shape(h, d), shape(h, d)],
        in_specs=[SMEM] + [VM] * 13, out_specs=[VM] * 4, scratch_shapes=[pltpu.VMEM((n, d), BF)],
        compiler_params=params(), cost_estimate=cost(8 * n * d * d, 8 * n * d), name="middle")(
            flag, state, q, k, v, before, after, table, wk, wv, wo, other, gain, halo)

def last(state, q, k, v, before, after, table, wk, wv, wo):
    n, d = state.shape
    return pl.pallas_call(last_body, out_shape=shape(n, d),
        in_specs=[VM] * 10, out_specs=VM, scratch_shapes=[pltpu.VMEM((n, d), BF)],
        compiler_params=params(), cost_estimate=cost(8 * n * d * d, 8 * n * d), name="last")(
            state, q, k, v, before, after, table, wk, wv, wo)


def per_device(states, entering, norm_gain, wq, wk, wv, wo, senders, halo_rows):
    lead = lax.axis_index("lead")
    gain = norm_gain[None]
    halo = halo_rows[0]
    forward = [(i, (i + 1) % 16) for i in range(lax.axis_size("mesh"))]
    backward = [(b, a) for a, b in forward]
    leads = lax.axis_size("lead")
    route = [(i, (i + 2) % leads) for i in range(leads)]

    def is_lead(index):
        return (lead == index).astype(jnp.int32)[None]

    def swapped(low, high):
        return lax.ppermute(high, "mesh", forward), lax.ppermute(low, "mesh", backward)

    def first_half(state, member, at, senders=None):
        return prep(is_lead(at), state, entering[0, member], gain, halo, senders)

    far = lax.ppermute(states[0, 0], "lead", route)
    state, normed, low, high, table = first_half(states[0, 1], 1, leads - 1, senders)

    def advance_twice(state, normed, low, high, member, at):
        before, after = swapped(low, high)
        q, k, v = project(normed, wq, wk, wv)
        state, normed, low, high = middle(
            is_lead(at), state, q, k, v, before, after, table, wk, wv, wo, entering[1, member], gain, halo)
        before, after = swapped(low, high)
        q, k, v = project(normed, wq, wk, wv)
        return last(state, q, k, v, before, after, table, wk, wv, wo)

    near = advance_twice(state, normed, low, high, 1, leads - 2)
    done_far = lax.ppermute(near, "lead", route)
    state, normed, low, high = first_half(far, 0, 1)
    here = advance_twice(state, normed, low, high, 0, 0)
    return jnp.stack([here, done_far])[None]


def solution(mesh):
    P = jax.sharding.PartitionSpec
    in_specs = (
        P("lead", None, "mesh", None),
        P(None, None, "mesh", None),
        P(),
        P(),
        P(),
        P(),
        P(),
        P("mesh", None),
        P("mesh", None, None),
    )
    return jax.shard_map(
        per_device, mesh=mesh, in_specs=in_specs, out_specs=P("lead", None, "mesh", None), check_vma=False
    )
```

```python
import functools

import jax
import jax.numpy as jnp
from jax import lax
from jax.experimental import pallas as pl
from jax.experimental.pallas import tpu as pltpu

HEAD_DIM = 64
LANES = 128
NEVER = -1e30
BF = jnp.bfloat16
F32 = jnp.float32
VMEM_BYTES = 16 * 1024 * 1024
VMEM = pl.BlockSpec(memory_space=pltpu.VMEM)
HBM = pl.BlockSpec(memory_space=pltpu.HBM)
ANY = pl.BlockSpec(memory_space=pl.ANY)


def shape(*dims, dtype=BF):
    return jax.ShapeDtypeStruct(dims, dtype)


def call(body, name, ins, specs, outs, out_specs, scratch=(), micros=1.0, **more):
    return pl.pallas_call(
        body,
        out_shape=outs,
        in_specs=specs,
        out_specs=out_specs,
        scratch_shapes=list(scratch),
        compiler_params=pltpu.CompilerParams(vmem_limit_bytes=VMEM_BYTES),
        cost_estimate=pl.CostEstimate(flops=int(micros * 1e9), bytes_accessed=1000, transcendentals=0),
        name=name,
        **more,
    )(*ins)


def normalised(x, gain):
    values = x.astype(F32)
    centred = values - jnp.mean(values, axis=-1, keepdims=True)
    spread = jnp.mean(centred * centred, axis=-1, keepdims=True)
    return (centred * lax.rsqrt(spread + 1e-05) * gain).astype(BF)


def rows_of(table, indices):
    spots = lax.broadcasted_iota(jnp.int32, (table.shape[0], indices.shape[1]), 0)
    picks = jnp.where(spots == indices, 1.0, 0.0)
    return jnp.dot(picks.T.astype(BF), table, preferred_element_type=F32).astype(BF)


def begin(chosen, gain, halo, odd, state, normed, cross, inner):
    state[...] = chosen
    rows = normalised(chosen, gain[...])
    normed[...] = rows
    low, high = halo[0:1], halo[1:2]
    cross[...] = rows_of(rows, jnp.where(odd == 1, high, low))
    inner[...] = rows_of(rows, jnp.where(odd == 1, low, high))


def bias_table(senders, odd, table):
    nodes = table.shape[0]
    count = jnp.zeros((table.shape[1], nodes), F32)
    spots = lax.broadcasted_iota(jnp.int32, count.shape, 0)
    half = (table.shape[1] - nodes) // 2
    spots = jnp.where((spots >= nodes) & (odd == 1), jnp.where(spots >= nodes + half, spots - half, spots + half), spots)
    for j in range(senders.shape[0]):
        count += jnp.where(spots == senders[j:j + 1], 1.0, 0.0)
    table[...] = jnp.where(count > 0, jnp.log(count), NEVER).T


def place_of(index):
    return lax.axis_index("lead") == index, lax.rem(lax.axis_index("mesh"), 2)


def near_first_body(index, states, entering, all_gain, all_halo, all_senders,
                    state, normed, cross, inner, table, far, own, gain, halo, senders, sems):
    special, odd = place_of(index)
    small = [
        pltpu.make_async_copy(source, target, sems.at[2 + i])
        for i, (source, target) in enumerate(((all_senders, senders), (all_halo, halo), (all_gain, gain)))
    ]
    for copy in small:
        copy.start()

    @pl.when(special)
    def _():
        pltpu.make_async_copy(entering.at[0, 1], own, sems.at[1]).start()

    @pl.when(jnp.logical_not(special))
    def _():
        pltpu.make_async_copy(states.at[0, 1], own, sems.at[1]).start()

    to_far = pltpu.make_async_copy(states.at[0, 0], far, sems.at[0])
    to_far.start()
    for copy in small:
        copy.wait()
    bias_table(senders, odd, table)
    pltpu.make_async_copy(states.at[0, 1], own, sems.at[1]).wait()
    begin(own[...], gain, halo, odd, state, normed, cross, inner)
    to_far.wait()


def far_first_body(index, moved, entering, gain, halo, token, state, normed, cross, inner, own, sem):
    special, odd = place_of(index)
    copy = pltpu.make_async_copy(entering.at[0, 0], own, sem)

    @pl.when(special)
    def _():
        copy.start()
        copy.wait()

    begin(jnp.where(special, own[...], moved[...]), gain, halo, odd, state, normed, cross, inner)


def stream_body(normed, wq, wk, wv, wo, q, k, v, vq, vk, vv, vo, sems):
    copies = [
        pltpu.make_async_copy(source, target, sems.at[i])
        for i, (source, target) in enumerate(((wk, vk), (wv, vv), (wq, vq), (wo, vo)))
    ]
    for copy in copies:
        copy.start()
    rows = normed[...]
    copies[0].wait()
    k[...] = jnp.dot(rows, vk[...], preferred_element_type=F32).astype(BF)
    copies[1].wait()
    v[...] = jnp.dot(rows, vv[...], preferred_element_type=F32).astype(BF)
    copies[2].wait()
    q[...] = jnp.dot(rows, vq[...], preferred_element_type=F32).astype(BF) * BF(HEAD_DIM ** -0.5)
    copies[3].wait()


def project_body(normed, wq, wk, wv, q, k, v):
    rows = normed[...]
    q[...] = jnp.dot(rows, wq[...], preferred_element_type=F32).astype(BF) * BF(HEAD_DIM ** -0.5)
    k[...] = jnp.dot(rows, wk[...], preferred_element_type=F32).astype(BF)
    v[...] = jnp.dot(rows, wv[...], preferred_element_type=F32).astype(BF)


def attend(state, q, k, v, cross, inner, table, wk, wv, wo, attended):
    halo = jnp.concatenate([cross[...], inner[...]], axis=0)
    more_k = jnp.dot(halo, wk[...], preferred_element_type=F32).astype(BF)
    more_v = jnp.dot(halo, wv[...], preferred_element_type=F32).astype(BF)
    bias = table[...]
    nodes, width = q.shape
    bias = jnp.concatenate([bias, bias], axis=0)
    first = lax.broadcasted_iota(jnp.int32, (nodes, LANES), 1) < HEAD_DIM
    ones = jnp.ones((table.shape[1], LANES), BF)
    for i in range(width // LANES):
        at = slice(i * LANES, (i + 1) * LANES)
        pair = q[:, at]
        zero = jnp.zeros_like(pair)
        both = jnp.concatenate([jnp.where(first, pair, zero), jnp.where(first, zero, pair)], axis=0)
        keys = jnp.concatenate([k[:, at], more_k[:, at]], axis=0)
        values = jnp.concatenate([v[:, at], more_v[:, at]], axis=0)
        scores = lax.dot_general(both, keys, (((1,), (1,)), ((), ())), preferred_element_type=F32) + bias
        expo = jnp.exp(scores - jnp.max(scores, axis=1, keepdims=True)).astype(BF)
        sums = jnp.dot(expo, jnp.concatenate([values, ones], axis=1), preferred_element_type=F32)
        top = sums[:nodes, :LANES] / sums[:nodes, LANES:]
        low = sums[nodes:, :LANES] / sums[nodes:, LANES:]
        attended[:, at] = jnp.where(first, top, low).astype(BF)
    update = jnp.dot(attended[...], wo[...], preferred_element_type=F32)
    return (state[...].astype(F32) + update).astype(BF)


def middle_of(member, index):
    def body(state, q, k, v, cross, inner, table, wk, wv, wo, entering, gain, halo, token,
             new_state, normed, new_cross, new_inner, attended, own, sem):
        special, odd = place_of(index)
        copy = pltpu.make_async_copy(entering.at[1, member], own, sem)

        @pl.when(special)
        def _():
            copy.start()

        moved = attend(state, q, k, v, cross, inner, table, wk, wv, wo, attended)

        @pl.when(special)
        def _():
            copy.wait()

        begin(jnp.where(special, own[...], moved), gain, halo, odd, new_state, normed, new_cross, new_inner)

    return body


def last_body(state, q, k, v, cross, inner, table, wk, wv, wo, token, out, attended):
    out[...] = attend(state, q, k, v, cross, inner, table, wk, wv, wo, attended)


def last_out_body(state, q, k, v, cross, inner, table, wk, wv, wo, out, attended, result, sem):
    result[...] = attend(state, q, k, v, cross, inner, table, wk, wv, wo, attended)
    copy = pltpu.make_async_copy(result, out.at[0, 0], sem)
    copy.start()
    copy.wait()


def join_body(whole, arrived, out, sem):
    copy = pltpu.make_async_copy(arrived, out.at[0, 1], sem)
    copy.start()
    copy.wait()


def per_device(states, entering, norm_gain, wq, wk, wv, wo, senders, halo_rows):
    leads, places = lax.axis_size("lead"), lax.axis_size("mesh")
    members, nodes, width = states.shape[1:]
    edge = halo_rows.shape[2]
    gain, halo, senders = norm_gain[None], halo_rows[0], senders.T
    states, entering, wq, wk, wv, wo = (
        pltpu.with_memory_space_constraint(x, pltpu.HBM) for x in (states, entering, wq, wk, wv, wo)
    )
    inner_route = [(i, i ^ 1) for i in range(places)]
    partner = [min(max(((i - 1) ^ 1) + 1, 0), places - 1) if 0 < i < places - 1 else i for i in range(places)]
    cross_route = list(enumerate(partner))
    route = [(i, (i + 2) % leads) for i in range(leads)]
    block, rim = shape(nodes, width), shape(edge, width)
    weight = shape(width, width)
    begun, begun_specs = [block, block, rim, rim], [VMEM] * 4
    dma = pltpu.SemaphoreType.DMA

    def exchanged(cross, inner):
        return lax.ppermute(cross, "mesh", cross_route), lax.ppermute(inner, "mesh", inner_route)

    def project(normed):
        return call(project_body, "project", [normed, vq, vk, vv], [VMEM] * 4, [block] * 3, [VMEM] * 3)

    def middle(member, index, state, q, k, v, cross, inner, token):
        return call(
            middle_of(member, index), f"middle_{member}",
            [state, q, k, v, cross, inner, table, vk, vv, vo, entering, gain, halo, token],
            [VMEM] * 10 + [HBM, VMEM, VMEM, ANY], begun, begun_specs,
            [pltpu.VMEM((nodes, width), BF), pltpu.VMEM((nodes, width), BF), dma],
        )

    state1, normed1, cross1, inner1, table, far = call(
        functools.partial(near_first_body, leads - 1), "near_first",
        [states, entering] + [pltpu.with_memory_space_constraint(x, pltpu.HBM) for x in (gain, halo, senders)],
        [HBM] * 5,
        begun + [shape(nodes, nodes + 2 * edge, dtype=F32), block], begun_specs + [VMEM] * 2,
        [pltpu.VMEM((nodes, width), BF)] + [pltpu.VMEM(x.shape, x.dtype) for x in (gain, halo, senders)] + [dma((5,))],
    )
    far = lax.ppermute(far, "lead", route)
    cross1, inner1 = exchanged(cross1, inner1)
    q1, k1, v1, vq, vk, vv, vo = call(
        stream_body, "stream", [normed1, wq, wk, wv, wo], [VMEM] + [HBM] * 4,
        [block] * 3 + [weight] * 4, [VMEM] * 7, [dma((4,))],
    )
    state1, normed1, cross1, inner1 = middle(1, leads - 2, state1, q1, k1, v1, cross1, inner1, k1)
    cross1, inner1 = exchanged(cross1, inner1)
    q1, k1, v1 = project(normed1)
    state0, normed0, cross0, inner0 = call(
        functools.partial(far_first_body, 1), "far_first",
        [far, entering, gain, halo, k1],
        [VMEM, HBM, VMEM, VMEM, ANY], begun, begun_specs,
        [pltpu.VMEM((nodes, width), BF), dma],
    )
    token = cross0
    cross0, inner0 = exchanged(cross0, inner0)
    near = call(
        last_body, "last_1",
        [state1, q1, k1, v1, cross1, inner1, table, vk, vv, vo, token],
        [VMEM] * 10 + [ANY], block, VMEM, [pltpu.VMEM((nodes, width), BF)],
    )
    arrived = lax.ppermute(near, "lead", route)
    q0, k0, v0 = project(normed0)
    state0, normed0, cross0, inner0 = middle(0, 0, state0, q0, k0, v0, cross0, inner0, near)
    cross0, inner0 = exchanged(cross0, inner0)
    q0, k0, v0 = project(normed0)
    whole = call(
        last_out_body, "last_0",
        [state0, q0, k0, v0, cross0, inner0, table, vk, vv, vo],
        [VMEM] * 10, shape(1, members, nodes, width), HBM,
        [pltpu.VMEM((nodes, width), BF), pltpu.VMEM((nodes, width), BF), dma],
    )
    return call(
        join_body, "join", [whole, arrived], [HBM, VMEM],
        shape(1, members, nodes, width), HBM, [dma], input_output_aliases={0: 0},
    )


def solution(mesh):
    P = jax.sharding.PartitionSpec
    in_specs = (
        P("lead", None, "mesh", None),
        P(None, None, "mesh", None),
        P(),
        P(),
        P(),
        P(),
        P(),
        P("mesh", None),
        P("mesh", None, None),
    )
    return jax.shard_map(
        per_device, mesh=mesh, in_specs=in_specs, out_specs=P("lead", None, "mesh", None), check_vma=False
    )
```

```python
import functools

import jax
import jax.numpy as jnp
from jax import lax
from jax.experimental import pallas as pl
from jax.experimental.pallas import tpu as pltpu

HEAD_DIM = 64
LANES = 128
NEVER = -1e30
BF = jnp.bfloat16
F32 = jnp.float32
VMEM_BYTES = 16 * 1024 * 1024
VMEM = pl.BlockSpec(memory_space=pltpu.VMEM)
HBM = pl.BlockSpec(memory_space=pltpu.HBM)
ANY = pl.BlockSpec(memory_space=pl.ANY)


def shape(*dims, dtype=BF):
    return jax.ShapeDtypeStruct(dims, dtype)


def call(body, name, ins, specs, outs, out_specs, scratch=(), micros=1.0, **more):
    return pl.pallas_call(
        body,
        out_shape=outs,
        in_specs=specs,
        out_specs=out_specs,
        scratch_shapes=list(scratch),
        compiler_params=pltpu.CompilerParams(vmem_limit_bytes=VMEM_BYTES),
        cost_estimate=pl.CostEstimate(flops=int(micros * 1e9), bytes_accessed=1000, transcendentals=0),
        name=name,
        **more,
    )(*ins)


def normalised(x, gain):
    values = x.astype(F32)
    centred = values - jnp.mean(values, axis=-1, keepdims=True)
    spread = jnp.mean(centred * centred, axis=-1, keepdims=True)
    return (centred * lax.rsqrt(spread + 1e-05) * gain).astype(BF)


def rows_of(table, indices):
    spots = lax.broadcasted_iota(jnp.int32, (table.shape[0], indices.shape[1]), 0)
    picks = jnp.where(spots == indices, 1.0, 0.0)
    return jnp.dot(picks.T.astype(BF), table, preferred_element_type=F32).astype(BF)


def begin(chosen, gain, halo, odd, state, normed, cross, inner):
    state[...] = chosen
    rows = normalised(chosen, gain[...])
    normed[...] = rows
    low, high = halo[0:1], halo[1:2]
    cross[...] = rows_of(rows, jnp.where(odd == 1, high, low))
    inner[...] = rows_of(rows, jnp.where(odd == 1, low, high))


def bias_table(senders, odd, table):
    nodes = table.shape[0]
    count = jnp.zeros((table.shape[1], nodes), F32)
    spots = lax.broadcasted_iota(jnp.int32, count.shape, 0)
    half = (table.shape[1] - nodes) // 2
    spots = jnp.where((spots >= nodes) & (odd == 1), jnp.where(spots >= nodes + half, spots - half, spots + half), spots)
    for j in range(senders.shape[0]):
        count += jnp.where(spots == senders[j:j + 1], 1.0, 0.0)
    table[...] = jnp.where(count > 0, jnp.log(count), NEVER).T


def place_of(index):
    return lax.axis_index("lead") == index, lax.rem(lax.axis_index("mesh"), 2)


def fetch_body(states, far, sem):
    copy = pltpu.make_async_copy(states.at[0, 0], far, sem)
    copy.start()
    copy.wait()


def near_first_body(index, states, entering, all_gain, all_halo, all_senders, token,
                    state, normed, cross, inner, table, own, gain, halo, senders, sems):
    special, odd = place_of(index)
    small = [
        pltpu.make_async_copy(source, target, sems.at[2 + i])
        for i, (source, target) in enumerate(((all_senders, senders), (all_halo, halo), (all_gain, gain)))
    ]
    for copy in small:
        copy.start()

    @pl.when(special)
    def _():
        pltpu.make_async_copy(entering.at[0, 1], own, sems.at[1]).start()

    @pl.when(jnp.logical_not(special))
    def _():
        pltpu.make_async_copy(states.at[0, 1], own, sems.at[1]).start()

    for copy in small:
        copy.wait()
    bias_table(senders, odd, table)
    pltpu.make_async_copy(states.at[0, 1], own, sems.at[1]).wait()
    begin(own[...], gain, halo, odd, state, normed, cross, inner)


def far_first_body(index, moved, entering, gain, halo, token, state, normed, cross, inner, own, sem):
    special, odd = place_of(index)
    copy = pltpu.make_async_copy(entering.at[0, 0], own, sem)

    @pl.when(special)
    def _():
        copy.start()
        copy.wait()

    begin(jnp.where(special, own[...], moved[...]), gain, halo, odd, state, normed, cross, inner)


def stream_body(normed, wq, wk, wv, wo, q, k, v, vq, vk, vv, vo, sems):
    copies = [
        pltpu.make_async_copy(source, target, sems.at[i])
        for i, (source, target) in enumerate(((wk, vk), (wv, vv), (wq, vq), (wo, vo)))
    ]
    for copy in copies:
        copy.start()
    rows = normed[...]
    copies[0].wait()
    k[...] = jnp.dot(rows, vk[...], preferred_element_type=F32).astype(BF)
    copies[1].wait()
    v[...] = jnp.dot(rows, vv[...], preferred_element_type=F32).astype(BF)
    copies[2].wait()
    q[...] = jnp.dot(rows, vq[...], preferred_element_type=F32).astype(BF) * BF(HEAD_DIM ** -0.5)
    copies[3].wait()


def project_body(normed, wq, wk, wv, q, k, v):
    rows = normed[...]
    q[...] = jnp.dot(rows, wq[...], preferred_element_type=F32).astype(BF) * BF(HEAD_DIM ** -0.5)
    k[...] = jnp.dot(rows, wk[...], preferred_element_type=F32).astype(BF)
    v[...] = jnp.dot(rows, wv[...], preferred_element_type=F32).astype(BF)


def attention(q, k, v, cross, inner, table, wk, wv, attended):
    halo = jnp.concatenate([cross[...], inner[...]], axis=0)
    more_k = jnp.dot(halo, wk[...], preferred_element_type=F32).astype(BF)
    more_v = jnp.dot(halo, wv[...], preferred_element_type=F32).astype(BF)
    bias = table[...]
    nodes, width = q.shape
    bias = jnp.concatenate([bias, bias], axis=0)
    first = lax.broadcasted_iota(jnp.int32, (nodes, LANES), 1) < HEAD_DIM
    ones = jnp.ones((table.shape[1], LANES), BF)
    for i in range(width // LANES):
        at = slice(i * LANES, (i + 1) * LANES)
        pair = q[:, at]
        zero = jnp.zeros_like(pair)
        both = jnp.concatenate([jnp.where(first, pair, zero), jnp.where(first, zero, pair)], axis=0)
        keys = jnp.concatenate([k[:, at], more_k[:, at]], axis=0)
        values = jnp.concatenate([v[:, at], more_v[:, at]], axis=0)
        scores = lax.dot_general(both, keys, (((1,), (1,)), ((), ())), preferred_element_type=F32) + bias
        expo = jnp.exp(scores - jnp.max(scores, axis=1, keepdims=True)).astype(BF)
        sums = jnp.dot(expo, jnp.concatenate([values, ones], axis=1), preferred_element_type=F32)
        top = sums[:nodes, :LANES] / sums[:nodes, LANES:]
        low = sums[nodes:, :LANES] / sums[nodes:, LANES:]
        attended[:, at] = jnp.where(first, top, low).astype(BF)


def updated(state, attended, wo):
    update = jnp.dot(attended[...], wo[...], preferred_element_type=F32)
    return (state[...].astype(F32) + update).astype(BF)


def attend(state, q, k, v, cross, inner, table, wk, wv, wo, attended):
    attention(q, k, v, cross, inner, table, wk, wv, attended)
    return updated(state, attended, wo)


def middle_of(member, index):
    def body(state, q, k, v, cross, inner, table, wk, wv, wo, entering, gain, halo, token,
             new_state, normed, new_cross, new_inner, attended, own, sem):
        special, odd = place_of(index)
        copy = pltpu.make_async_copy(entering.at[1, member], own, sem)

        @pl.when(special)
        def _():
            copy.start()

        moved = attend(state, q, k, v, cross, inner, table, wk, wv, wo, attended)

        @pl.when(special)
        def _():
            copy.wait()

        begin(jnp.where(special, own[...], moved), gain, halo, odd, new_state, normed, new_cross, new_inner)

    return body


def last_body(state, q, k, v, cross, inner, table, wk, wv, wo, token, out, attended):
    out[...] = attend(state, q, k, v, cross, inner, table, wk, wv, wo, attended)


def last_0_body(q, k, v, cross, inner, table, wk, wv, attended):
    attention(q, k, v, cross, inner, table, wk, wv, attended)


def finish_body(state, attended, wo, arrived, out, result, sems):
    there = pltpu.make_async_copy(arrived, out.at[0, 1], sems.at[0])
    there.start()
    result[...] = updated(state, attended, wo)
    here = pltpu.make_async_copy(result, out.at[0, 0], sems.at[1])
    here.start()
    there.wait()
    here.wait()


def per_device(states, entering, norm_gain, wq, wk, wv, wo, senders, halo_rows):
    leads, places = lax.axis_size("lead"), lax.axis_size("mesh")
    members, nodes, width = states.shape[1:]
    edge = halo_rows.shape[2]
    gain, halo, senders = norm_gain[None], halo_rows[0], senders.T
    states, entering, wq, wk, wv, wo = (
        pltpu.with_memory_space_constraint(x, pltpu.HBM) for x in (states, entering, wq, wk, wv, wo)
    )
    inner_route = [(i, i ^ 1) for i in range(places)]
    cross_route = [(i, (((i - 1) ^ 1) + 1) % places) for i in range(places)]
    route = [(i, (i + 2) % leads) for i in range(leads)]
    block, rim = shape(nodes, width), shape(edge, width)
    weight = shape(width, width)
    begun, begun_specs = [block, block, rim, rim], [VMEM] * 4
    dma = pltpu.SemaphoreType.DMA

    def exchanged(cross, inner):
        return lax.ppermute(cross, "mesh", cross_route), lax.ppermute(inner, "mesh", inner_route)

    def project(normed):
        return call(project_body, "project", [normed, vq, vk, vv], [VMEM] * 4, [block] * 3, [VMEM] * 3)

    def middle(member, index, state, q, k, v, cross, inner, token):
        return call(
            middle_of(member, index), f"middle_{member}",
            [state, q, k, v, cross, inner, table, vk, vv, vo, entering, gain, halo, token],
            [VMEM] * 10 + [HBM, VMEM, VMEM, ANY], begun, begun_specs,
            [pltpu.VMEM((nodes, width), BF), pltpu.VMEM((nodes, width), BF), dma],
        )

    far = call(fetch_body, "fetch", [states], [HBM], block, VMEM, [dma])
    token = far
    far = lax.ppermute(far, "lead", route)
    state1, normed1, cross1, inner1, table = call(
        functools.partial(near_first_body, leads - 1), "near_first",
        [states, entering] + [pltpu.with_memory_space_constraint(x, pltpu.HBM) for x in (gain, halo, senders)] + [token],
        [HBM] * 5 + [ANY],
        begun + [shape(nodes, nodes + 2 * edge, dtype=F32)], begun_specs + [VMEM],
        [pltpu.VMEM((nodes, width), BF)] + [pltpu.VMEM(x.shape, x.dtype) for x in (gain, halo, senders)] + [dma((5,))],
    )
    cross1, inner1 = exchanged(cross1, inner1)
    q1, k1, v1, vq, vk, vv, vo = call(
        stream_body, "stream", [normed1, wq, wk, wv, wo], [VMEM] + [HBM] * 4,
        [block] * 3 + [weight] * 4, [VMEM] * 7, [dma((4,))],
    )
    state1, normed1, cross1, inner1 = middle(1, leads - 2, state1, q1, k1, v1, cross1, inner1, k1)
    cross1, inner1 = exchanged(cross1, inner1)
    q1, k1, v1 = project(normed1)
    state0, normed0, cross0, inner0 = call(
        functools.partial(far_first_body, 1), "far_first",
        [far, entering, gain, halo, k1],
        [VMEM, HBM, VMEM, VMEM, ANY], begun, begun_specs,
        [pltpu.VMEM((nodes, width), BF), dma],
    )
    token = cross0
    cross0, inner0 = exchanged(cross0, inner0)
    near = call(
        last_body, "last_1",
        [state1, q1, k1, v1, cross1, inner1, table, vk, vv, vo, token],
        [VMEM] * 10 + [ANY], block, VMEM, [pltpu.VMEM((nodes, width), BF)],
    )
    arrived = lax.ppermute(near, "lead", route)
    q0, k0, v0 = project(normed0)
    state0, normed0, cross0, inner0 = middle(0, 0, state0, q0, k0, v0, cross0, inner0, near)
    cross0, inner0 = exchanged(cross0, inner0)
    q0, k0, v0 = project(normed0)
    attended = call(
        last_0_body, "last_0", [q0, k0, v0, cross0, inner0, table, vk, vv], [VMEM] * 8, block, VMEM,
    )
    return call(
        finish_body, "finish", [state0, attended, vo, arrived], [VMEM] * 4,
        shape(1, members, nodes, width), HBM, [pltpu.VMEM((nodes, width), BF), dma((2,))],
    )


def solution(mesh):
    P = jax.sharding.PartitionSpec
    in_specs = (
        P("lead", None, "mesh", None),
        P(None, None, "mesh", None),
        P(),
        P(),
        P(),
        P(),
        P(),
        P("mesh", None),
        P("mesh", None, None),
    )
    return jax.shard_map(
        per_device, mesh=mesh, in_specs=in_specs, out_specs=P("lead", None, "mesh", None), check_vma=False
    )
```

```python
import functools

import jax
import jax.numpy as jnp
from jax import lax
from jax.experimental import pallas as pl
from jax.experimental.pallas import tpu as pltpu

HEAD_DIM = 64
LANES = 128
NEVER = -1e30
BF = jnp.bfloat16
F32 = jnp.float32
CHUNKS = 4
VMEM_BYTES = 16 * 1024 * 1024
VMEM = pl.BlockSpec(memory_space=pltpu.VMEM)
HBM = pl.BlockSpec(memory_space=pltpu.HBM)
ANY = pl.BlockSpec(memory_space=pl.ANY)


def shape(*dims, dtype=BF):
    return jax.ShapeDtypeStruct(dims, dtype)


def call(body, name, ins, specs, outs, out_specs, scratch=(), micros=1.0, **more):
    return pl.pallas_call(
        body,
        out_shape=outs,
        in_specs=specs,
        out_specs=out_specs,
        scratch_shapes=list(scratch),
        compiler_params=pltpu.CompilerParams(vmem_limit_bytes=VMEM_BYTES),
        cost_estimate=pl.CostEstimate(flops=int(micros * 1e9), bytes_accessed=1000, transcendentals=0),
        name=name,
        **more,
    )(*ins)


def normalised(x, gain):
    values = x.astype(F32)
    centred = values - jnp.mean(values, axis=-1, keepdims=True)
    spread = jnp.mean(centred * centred, axis=-1, keepdims=True)
    return (centred * lax.rsqrt(spread + 1e-05) * gain).astype(BF)


def rows_of(table, indices):
    spots = lax.broadcasted_iota(jnp.int32, (table.shape[0], indices.shape[1]), 0)
    picks = jnp.where(spots == indices, 1.0, 0.0)
    return jnp.dot(picks.T.astype(BF), table, preferred_element_type=F32).astype(BF)


def begin(chosen, gain, halo, odd, state, normed, cross, inner):
    if state is not None:
        state[...] = chosen
    rows = normalised(chosen, gain[...])
    normed[...] = rows
    low, high = halo[0:1], halo[1:2]
    first, second = jnp.where(odd == 1, high, low), jnp.where(odd == 1, low, high)
    picked = rows_of(rows, jnp.concatenate([first, second], axis=1))
    cross[...] = picked[:halo.shape[1]]
    inner[...] = picked[halo.shape[1]:]


def bias_table(senders, odd, table):
    nodes = table.shape[0]
    count = jnp.zeros((table.shape[1], nodes), F32)
    spots = lax.broadcasted_iota(jnp.int32, count.shape, 0)
    half = (table.shape[1] - nodes) // 2
    spots = jnp.where((spots >= nodes) & (odd == 1), jnp.where(spots >= nodes + half, spots - half, spots + half), spots)
    for j in range(senders.shape[0]):
        count += jnp.where(spots == senders[j:j + 1], 1.0, 0.0)
    table[...] = jnp.where(count > 0, jnp.log(count), NEVER).T


def place_of(index):
    return lax.axis_index("lead") == index, lax.rem(lax.axis_index("mesh"), 2)


def fetch_body(index, states, entering, all_gain, all_halo, all_senders, far, own, gain, halo, senders, sems):
    special, _ = place_of(index)
    pairs = ((states.at[0, 0], far), (all_gain, gain), (all_halo, halo), (all_senders, senders), (states.at[0, 1], own))
    copies = [pltpu.make_async_copy(source, target, sems.at[i]) for i, (source, target) in enumerate(pairs)]
    for copy in copies[:-1]:
        copy.start()

    @pl.when(special)
    def _():
        pltpu.make_async_copy(entering.at[0, 1], own, sems.at[4]).start()

    @pl.when(jnp.logical_not(special))
    def _():
        copies[4].start()

    for copy in copies:
        copy.wait()


def near_first_body(own, gain, halo, senders, normed, cross, inner, table):
    odd = place_of(0)[1]
    bias_table(senders, odd, table)
    begin(own[...], gain, halo, odd, None, normed, cross, inner)


def far_first_body(index, moved, entering, gain, halo, token, state, normed, cross, inner, own, sem):
    special, odd = place_of(index)
    copy = pltpu.make_async_copy(entering.at[0, 0], own, sem)

    @pl.when(special)
    def _():
        copy.start()
        copy.wait()

    begin(jnp.where(special, own[...], moved[...]), gain, halo, odd, state, normed, cross, inner)


def queries_of(rows, weight):
    return jnp.dot(rows, weight, preferred_element_type=F32).astype(BF) * BF(HEAD_DIM ** -0.5)


def stream_body(normed, wq, wk, wv, wo, q, vq, vk, vv, vo, sems):
    copies = []
    for i, (source, target) in enumerate(((wq, vq), (wk, vk), (wv, vv), (wo, vo))):
        depth = source.shape[0] // CHUNKS
        for j in range(CHUNKS):
            at = pl.ds(j * depth, depth)
            copies.append(pltpu.make_async_copy(source.at[at], target.at[at], sems.at[i, j]))
            copies[-1].start()
    for copy in copies[:CHUNKS]:
        copy.wait()
    q[...] = queries_of(normed[...], vq[...])
    for copy in copies[CHUNKS:]:
        copy.wait()


def project_body(normed, wq, q):
    q[...] = queries_of(normed[...], wq[...])


def attention(q, normed, cross, inner, table, wk, wv, attended):
    rows = jnp.concatenate([normed[...], cross[...], inner[...]], axis=0)
    k = jnp.dot(rows, wk[...], preferred_element_type=F32).astype(BF)
    v = jnp.dot(rows, wv[...], preferred_element_type=F32).astype(BF)
    bias = table[...]
    nodes, width = q.shape
    bias = jnp.concatenate([bias, bias], axis=0)
    first = lax.broadcasted_iota(jnp.int32, (nodes, LANES), 1) < HEAD_DIM
    ones = jnp.ones((table.shape[1], LANES), BF)
    for i in range(width // LANES):
        at = slice(i * LANES, (i + 1) * LANES)
        pair = q[:, at]
        zero = jnp.zeros_like(pair)
        both = jnp.concatenate([jnp.where(first, pair, zero), jnp.where(first, zero, pair)], axis=0)
        keys, values = k[:, at], v[:, at]
        scores = lax.dot_general(both, keys, (((1,), (1,)), ((), ())), preferred_element_type=F32) + bias
        expo = jnp.exp(scores - jnp.max(scores, axis=1, keepdims=True)).astype(BF)
        sums = jnp.dot(expo, jnp.concatenate([values, ones], axis=1), preferred_element_type=F32)
        top = sums[:nodes, :LANES] / sums[:nodes, LANES:]
        low = sums[nodes:, :LANES] / sums[nodes:, LANES:]
        attended[:, at] = jnp.where(first, top, low).astype(BF)


def updated(state, attended, wo):
    update = jnp.dot(attended[...], wo[...], preferred_element_type=F32)
    return (state[...].astype(F32) + update).astype(BF)


def attend(state, q, normed, cross, inner, table, wk, wv, wo, attended):
    attention(q, normed, cross, inner, table, wk, wv, attended)
    return updated(state, attended, wo)


def middle_of(member, index):
    def body(state, q, normed, cross, inner, table, wk, wv, wo, entering, gain, halo, token,
             new_state, new_normed, new_cross, new_inner, attended, moved, sem):
        special, odd = place_of(index)

        @pl.when(special)
        def _():
            copy = pltpu.make_async_copy(entering.at[1, member], moved, sem)
            copy.start()
            copy.wait()

        @pl.when(jnp.logical_not(special))
        def _():
            moved[...] = attend(state, q, normed, cross, inner, table, wk, wv, wo, attended)

        begin(moved[...], gain, halo, odd, new_state, new_normed, new_cross, new_inner)

    return body


def last_body(state, q, normed, cross, inner, table, wk, wv, wo, token, out, attended):
    out[...] = attend(state, q, normed, cross, inner, table, wk, wv, wo, attended)


def finish_body(here, there, out, sems):
    copies = [pltpu.make_async_copy(x, out.at[0, i], sems.at[i]) for i, x in enumerate((here, there))]
    for copy in copies:
        copy.start()
    for copy in copies:
        copy.wait()


def per_device(states, entering, norm_gain, wq, wk, wv, wo, senders, halo_rows):
    leads, places = lax.axis_size("lead"), lax.axis_size("mesh")
    members, nodes, width = states.shape[1:]
    edge = halo_rows.shape[2]
    gain, halo, senders = norm_gain[None], halo_rows[0], senders.T
    states, entering = (pltpu.with_memory_space_constraint(x, pltpu.HBM) for x in (states, entering))
    vq, vk, vv, vo = wq, wk, wv, wo
    inner_route = [(i, i ^ 1) for i in range(places)]
    cross_route = [
        (a * places + i, ((a + leads // 2) % leads) * places + i if i in (0, places - 1) else a * places + ((i - 1) ^ 1) + 1)
        for a in range(leads)
        for i in range(places)
    ]
    route = [(i, (i + 2) % leads) for i in range(leads)]
    block, rim = shape(nodes, width), shape(edge, width)
    weight = shape(width, width)
    begun, begun_specs = [block, block, rim, rim], [VMEM] * 4
    dma = pltpu.SemaphoreType.DMA

    def exchanged(cross, inner):
        return lax.ppermute(cross, ("lead", "mesh"), cross_route), lax.ppermute(inner, "mesh", inner_route)

    def project(normed):
        return call(project_body, "project", [normed, vq], [VMEM] * 2, block, VMEM)

    def last(state, q, normed, cross, inner, token, name):
        return call(
            last_body, name, [state, q, normed, cross, inner, table, vk, vv, vo, token],
            [VMEM] * 9 + [ANY], block, VMEM, [pltpu.VMEM((nodes, width), BF)],
        )

    def middle(member, index, state, q, normed, cross, inner, token):
        return call(
            middle_of(member, index), f"middle_{member}",
            [state, q, normed, cross, inner, table, vk, vv, vo, entering, gain, halo, token],
            [VMEM] * 9 + [HBM, VMEM, VMEM, ANY], begun, begun_specs,
            [pltpu.VMEM((nodes, width), BF), pltpu.VMEM((nodes, width), BF), dma],
        )

    far, state1, gain, halo, senders = call(
        functools.partial(fetch_body, leads - 1), "fetch",
        [states, entering] + [pltpu.with_memory_space_constraint(x, pltpu.HBM) for x in (gain, halo, senders)],
        [HBM] * 5,
        [block, block] + [shape(*x.shape, dtype=x.dtype) for x in (gain, halo, senders)],
        [VMEM] * 5, [dma((5,))],
    )
    far = lax.ppermute(far, "lead", route)
    normed1, cross1, inner1, table = call(
        near_first_body, "near_first", [state1, gain, halo, senders], [VMEM] * 4,
        [block, rim, rim, shape(nodes, nodes + 2 * edge, dtype=F32)], [VMEM] * 4,
    )
    cross1, inner1 = exchanged(cross1, inner1)
    q1 = project(normed1)
    state1, normed1, cross1, inner1 = middle(1, leads - 2, state1, q1, normed1, cross1, inner1, q1)
    cross1, inner1 = exchanged(cross1, inner1)
    q1 = project(normed1)
    state0, normed0, cross0, inner0 = call(
        functools.partial(far_first_body, 1), "far_first",
        [far, entering, gain, halo, q1],
        [VMEM, HBM, VMEM, VMEM, ANY], begun, begun_specs,
        [pltpu.VMEM((nodes, width), BF), dma],
    )
    token = cross0
    cross0, inner0 = exchanged(cross0, inner0)
    near = last(state1, q1, normed1, cross1, inner1, token, "last_1")
    arrived = lax.ppermute(near, "lead", route)
    q0 = project(normed0)
    state0, normed0, cross0, inner0 = middle(0, 0, state0, q0, normed0, cross0, inner0, near)
    cross0, inner0 = exchanged(cross0, inner0)
    q0 = project(normed0)
    here = last(state0, q0, normed0, cross0, inner0, normed0, "last_0")
    return call(
        finish_body, "finish", [here, arrived], [VMEM] * 2,
        shape(1, members, nodes, width), HBM, [dma((2,))],
    )


def solution(mesh):
    P = jax.sharding.PartitionSpec
    in_specs = (
        P("lead", None, "mesh", None),
        P(None, None, "mesh", None),
        P(),
        P(),
        P(),
        P(),
        P(),
        P("mesh", None),
        P("mesh", None, None),
    )
    return jax.shard_map(
        per_device, mesh=mesh, in_specs=in_specs, out_specs=P("lead", None, "mesh", None), check_vma=False
    )
```

```python
import functools

import jax
import jax.numpy as jnp
from jax import lax
from jax.experimental import pallas as pl
from jax.experimental.pallas import tpu as pltpu

HEAD_DIM = 64
LANES = 128
NEVER = -1e30
BF = jnp.bfloat16
F32 = jnp.float32
CHUNKS = 4
MP = 1.0
ML = 1.0
VMEM_BYTES = 16 * 1024 * 1024
VMEM = pl.BlockSpec(memory_space=pltpu.VMEM)
HBM = pl.BlockSpec(memory_space=pltpu.HBM)
ANY = pl.BlockSpec(memory_space=pl.ANY)


def shape(*dims, dtype=BF):
    return jax.ShapeDtypeStruct(dims, dtype)


def call(body, name, ins, specs, outs, out_specs, scratch=(), micros=1.0, **more):
    return pl.pallas_call(
        body,
        out_shape=outs,
        in_specs=specs,
        out_specs=out_specs,
        scratch_shapes=list(scratch),
        compiler_params=pltpu.CompilerParams(vmem_limit_bytes=VMEM_BYTES),
        cost_estimate=pl.CostEstimate(flops=int(micros * 1e9), bytes_accessed=1000, transcendentals=0),
        name=name,
        **more,
    )(*ins)


def normalised(x, gain):
    values = x.astype(F32)
    centred = values - jnp.mean(values, axis=-1, keepdims=True)
    spread = jnp.mean(centred * centred, axis=-1, keepdims=True)
    return (centred * lax.rsqrt(spread + 1e-05) * gain).astype(BF)


def rows_of(table, indices):
    spots = lax.broadcasted_iota(jnp.int32, (table.shape[0], indices.shape[1]), 0)
    picks = jnp.where(spots == indices, 1.0, 0.0)
    return jnp.dot(picks.T.astype(BF), table, preferred_element_type=F32).astype(BF)


def picked_rows(rows, halo, odd):
    low, high = halo[0:1], halo[1:2]
    first, second = jnp.where(odd == 1, high, low), jnp.where(odd == 1, low, high)
    return rows_of(rows, jnp.concatenate([first, second], axis=1))


def bias_table(senders, odd, table):
    nodes = table.shape[0]
    count = jnp.zeros((table.shape[1], nodes), F32)
    spots = lax.broadcasted_iota(jnp.int32, count.shape, 0)
    half = (table.shape[1] - nodes) // 2
    spots = jnp.where((spots >= nodes) & (odd == 1), jnp.where(spots >= nodes + half, spots - half, spots + half), spots)
    for j in range(senders.shape[0]):
        count += jnp.where(spots == senders[j:j + 1], 1.0, 0.0)
    table[...] = jnp.where(count > 0, jnp.log(count), NEVER).T


def parity():
    return lax.rem(lax.axis_index("mesh"), 2)


def start_body(once, twice, states, entering, all_gain, all_halo,
               far, own, gain, halo, normed, cross, inner, sems):
    lead = lax.axis_index("lead")
    small = ((all_gain, gain), (all_halo, halo))
    copies = [pltpu.make_async_copy(source, target, sems.at[i]) for i, (source, target) in enumerate(small)]
    for copy in copies:
        copy.start()
    choices = (
        (lead == once, entering, 1),
        (lead == twice, entering, 0),
        ((lead != once) & (lead != twice), states, 0),
    )
    for chosen, source, step in choices:

        @pl.when(chosen)
        def _(source=source, step=step):
            pltpu.make_async_copy(source.at[step, 1], own, sems.at[3]).start()
            pltpu.make_async_copy(source.at[step, 0], far, sems.at[4]).start()

    for copy in copies:
        copy.wait()
    odd = parity()
    edge = halo.shape[1]
    pltpu.make_async_copy(states.at[0, 1], own, sems.at[3]).wait()
    rows = normalised(own[...], gain[...])
    normed[...] = rows
    picked = picked_rows(rows, halo, odd)
    cross[:edge], inner[...] = picked[:edge], picked[edge:]
    pltpu.make_async_copy(states.at[0, 0], far, sems.at[4]).wait()
    low, high = halo[0:1], halo[1:2]
    cross[edge:] = rows_of(normalised(far[...], gain[...]), jnp.where(odd == 1, high, low))


def queries_of(rows, weight):
    return jnp.dot(rows, weight, preferred_element_type=F32).astype(BF) * BF(HEAD_DIM ** -0.5)


def stream_body(normed, wq, wk, wv, wo, q, vq, vk, vv, vo, sems):
    copies = []
    for i, (source, target) in enumerate(((wq, vq), (wk, vk), (wv, vv), (wo, vo))):
        depth = source.shape[0] // CHUNKS
        for j in range(CHUNKS):
            at = pl.ds(j * depth, depth)
            copies.append(pltpu.make_async_copy(source.at[at], target.at[at], sems.at[i, j]))
            copies[-1].start()
    for copy in copies[:CHUNKS]:
        copy.wait()
    q[...] = queries_of(normed[...], vq[...])
    for copy in copies[CHUNKS:]:
        copy.wait()


def project_first_body(normed, wq, senders, q, vq, table, sems):
    depth = wq.shape[0] // CHUNKS
    copies = []
    for i in range(CHUNKS):
        at = pl.ds(i * depth, depth)
        copies.append(pltpu.make_async_copy(wq.at[at], vq.at[at], sems.at[i]))
        copies[-1].start()
    bias_table(senders, parity(), table)
    for copy in copies:
        copy.wait()
    q[...] = queries_of(normed[...], vq[...])


def project_body(normed, wq, q):
    q[...] = queries_of(normed[...], wq[...])


def far_first_body(far, gain, halo, token, normed, inner):
    rows = normalised(far[...], gain[...])
    normed[...] = rows
    low, high = halo[0:1], halo[1:2]
    inner[...] = rows_of(rows, jnp.where(parity() == 1, low, high))


def attention(q, normed, cross, inner, table, wk, wv, attended):
    rows = jnp.concatenate([normed[...], cross, inner], axis=0)
    k = jnp.dot(rows, wk[...], preferred_element_type=F32).astype(BF)
    v = jnp.dot(rows, wv[...], preferred_element_type=F32).astype(BF)
    bias = table[...]
    nodes, width = q.shape
    bias = jnp.concatenate([bias, bias], axis=0)
    first = lax.broadcasted_iota(jnp.int32, (nodes, LANES), 1) < HEAD_DIM
    ones = jnp.ones((table.shape[1], LANES), BF)
    for i in range(width // LANES):
        at = slice(i * LANES, (i + 1) * LANES)
        pair = q[:, at]
        zero = jnp.zeros_like(pair)
        both = jnp.concatenate([jnp.where(first, pair, zero), jnp.where(first, zero, pair)], axis=0)
        scores = lax.dot_general(both, k[:, at], (((1,), (1,)), ((), ())), preferred_element_type=F32) + bias
        expo = jnp.exp(scores - jnp.max(scores, axis=1, keepdims=True)).astype(BF)
        sums = jnp.dot(expo, jnp.concatenate([v[:, at], ones], axis=1), preferred_element_type=F32)
        top = sums[:nodes, :LANES] / sums[:nodes, LANES:]
        low = sums[nodes:, :LANES] / sums[nodes:, LANES:]
        attended[:, at] = jnp.where(first, top, low).astype(BF)


def attend(state, q, normed, cross, inner, table, wk, wv, wo, attended):
    attention(q, normed, cross, inner, table, wk, wv, attended)
    update = jnp.dot(attended[...], wo[...], preferred_element_type=F32)
    return (state[...].astype(F32) + update).astype(BF)


def middle_body(splits, state, q, normed, cross, inner, table, wk, wv, wo, gain, halo,
                new_state, new_normed, new_cross, new_inner, *rest):
    edge = halo.shape[1]
    if splits:
        later, attended = rest
        later[...] = cross[edge:]
    else:
        attended, = rest
    moved = attend(state, q, normed, cross[:edge], inner[...], table, wk, wv, wo, attended)
    new_state[...] = moved
    rows = normalised(moved, gain[...])
    new_normed[...] = rows
    picked = picked_rows(rows, halo, parity())
    new_cross[...] = picked[:edge]
    new_inner[...] = picked[edge:]


def last_body(index, state, q, normed, cross, inner, table, wk, wv, wo, out, attended):
    special = lax.axis_index("lead") == index

    @pl.when(special)
    def _():
        out[...] = state[...]

    @pl.when(jnp.logical_not(special))
    def _():
        out[...] = attend(state, q, normed, cross[...], inner[...], table, wk, wv, wo, attended)


def finish_body(here, there, out, sems):
    copies = [pltpu.make_async_copy(x, out.at[0, i], sems.at[i]) for i, x in enumerate((here, there))]
    for copy in copies:
        copy.start()
    for copy in copies:
        copy.wait()


def per_device(states, entering, norm_gain, wq, wk, wv, wo, senders, halo_rows):
    leads, places = lax.axis_size("lead"), lax.axis_size("mesh")
    members, nodes, width = states.shape[1:]
    edge = halo_rows.shape[2]
    gain, halo, senders = norm_gain[None], halo_rows[0], senders.T
    states, entering = (pltpu.with_memory_space_constraint(x, pltpu.HBM) for x in (states, entering))
    vk, vv, vo = wk, wv, wo
    inner_route = [(i, i ^ 1) for i in range(places)]
    cross_route = [
        (a * places + i, ((a + leads // 2) % leads) * places + i if i in (0, places - 1) else a * places + ((i - 1) ^ 1) + 1)
        for a in range(leads)
        for i in range(places)
    ]
    route = [(i, (i + 2) % leads) for i in range(leads)]
    block, rim, rims = shape(nodes, width), shape(edge, width), shape(2 * edge, width)
    dma = pltpu.SemaphoreType.DMA

    def crossed(cross):
        return lax.ppermute(cross, ("lead", "mesh"), cross_route)

    def swapped(inner):
        return lax.ppermute(inner, "mesh", inner_route)

    def project(normed):
        return call(project_body, "project", [normed, vq], [VMEM] * 2, block, VMEM, micros=MP)

    def middle(name, splits, state, q, normed, cross, inner):
        return call(
            functools.partial(middle_body, splits), name,
            [state, q, normed, cross, inner, table, vk, vv, vo, gain, halo], [VMEM] * 11,
            [block, block, rim, rim] + [rim] * splits, [VMEM] * (4 + splits), [pltpu.VMEM((nodes, width), BF)],
        )

    def last(name, index, state, q, normed, cross, inner):
        return call(
            functools.partial(last_body, index), name,
            [state, q, normed, cross, inner, table, vk, vv, vo], [VMEM] * 9,
            block, VMEM, [pltpu.VMEM((nodes, width), BF)], micros=ML,
        )

    far, state1, gain, halo, normed1, cross, inner = call(
        functools.partial(start_body, leads - 2, leads - 1), "start",
        [states, entering] + [pltpu.with_memory_space_constraint(x, pltpu.HBM) for x in (gain, halo)],
        [HBM] * 4,
        [block, block] + [shape(*x.shape, dtype=x.dtype) for x in (gain, halo)] + [block, rims, rim],
        [VMEM] * 7, [dma((5,))],
    )
    cross = crossed(cross)
    inner = swapped(inner)
    q1, vq, table = call(
        project_first_body, "project_first",
        [normed1, pltpu.with_memory_space_constraint(wq, pltpu.HBM), senders], [VMEM, HBM, VMEM],
        [block, shape(width, width), shape(nodes, nodes + 2 * edge, dtype=F32)], [VMEM] * 3, [dma((CHUNKS,))],
        micros=MP,
    )
    far = lax.ppermute(far, "lead", route)
    state1, normed1, cross1, inner1, halo0 = middle("middle_1", True, state1, q1, normed1, cross, inner)
    cross1 = crossed(cross1)
    inner1 = swapped(inner1)
    q1 = project(normed1)
    halo0 = lax.ppermute(halo0, "lead", route)
    near = last("last_1", leads - 2, state1, q1, normed1, cross1, inner1)
    arrived = lax.ppermute(near, "lead", route)
    normed0, inner0 = call(
        far_first_body, "far_first", [far, gain, halo, near], [VMEM] * 3 + [ANY], [block, rim], [VMEM] * 2,
    )
    inner0 = swapped(inner0)
    q0 = project(normed0)
    state0, normed0, cross0, inner0 = middle("middle_0", False, far, q0, normed0, halo0, inner0)
    cross0 = crossed(cross0)
    inner0 = swapped(inner0)
    q0 = project(normed0)
    here = last("last_0", 0, state0, q0, normed0, cross0, inner0)
    return call(
        finish_body, "finish", [here, arrived], [VMEM] * 2,
        shape(1, members, nodes, width), HBM, [dma((2,))],
    )


def solution(mesh):
    P = jax.sharding.PartitionSpec
    in_specs = (
        P("lead", None, "mesh", None),
        P(None, None, "mesh", None),
        P(),
        P(),
        P(),
        P(),
        P(),
        P("mesh", None),
        P("mesh", None, None),
    )
    return jax.shard_map(
        per_device, mesh=mesh, in_specs=in_specs, out_specs=P("lead", None, "mesh", None), check_vma=False
    )
```

```python
import functools

import jax
import jax.numpy as jnp
from jax import lax
from jax.experimental import pallas as pl
from jax.experimental.pallas import tpu as pltpu

HEAD_DIM = 64
LANES = 128
NEVER = -1e30
BF = jnp.bfloat16
F32 = jnp.float32
MS = 3.0
MP = 1.0
ML = 1.0
VMEM_BYTES = 16 * 1024 * 1024
VMEM = pl.BlockSpec(memory_space=pltpu.VMEM)
HBM = pl.BlockSpec(memory_space=pltpu.HBM)
ANY = pl.BlockSpec(memory_space=pl.ANY)


def shape(*dims, dtype=BF):
    return jax.ShapeDtypeStruct(dims, dtype)


def call(body, name, ins, specs, outs, out_specs, scratch=(), micros=1.0, **more):
    return pl.pallas_call(
        body,
        out_shape=outs,
        in_specs=specs,
        out_specs=out_specs,
        scratch_shapes=list(scratch),
        compiler_params=pltpu.CompilerParams(vmem_limit_bytes=VMEM_BYTES),
        cost_estimate=pl.CostEstimate(flops=int(micros * 1e9), bytes_accessed=1000, transcendentals=0),
        name=name,
        **more,
    )(*ins)


def normalised(x, gain):
    values = x.astype(F32)
    centred = values - jnp.mean(values, axis=-1, keepdims=True)
    spread = jnp.mean(centred * centred, axis=-1, keepdims=True)
    return (centred * lax.rsqrt(spread + 1e-05) * gain).astype(BF)


def rows_of(table, indices):
    spots = lax.broadcasted_iota(jnp.int32, (table.shape[0], indices.shape[1]), 0)
    picks = jnp.where(spots == indices, 1.0, 0.0)
    return jnp.dot(picks.T.astype(BF), table, preferred_element_type=F32).astype(BF)


def picked_rows(rows, halo, odd):
    low, high = halo[0:1], halo[1:2]
    first, second = jnp.where(odd == 1, high, low), jnp.where(odd == 1, low, high)
    return rows_of(rows, jnp.concatenate([first, second], axis=1))


def bias_table(senders, odd, table):
    nodes = table.shape[0]
    count = jnp.zeros((table.shape[1], nodes), F32)
    spots = lax.broadcasted_iota(jnp.int32, count.shape, 0)
    half = (table.shape[1] - nodes) // 2
    spots = jnp.where((spots >= nodes) & (odd == 1), jnp.where(spots >= nodes + half, spots - half, spots + half), spots)
    for j in range(senders.shape[0]):
        count += jnp.where(spots == senders[j:j + 1], 1.0, 0.0)
    table[...] = jnp.where(count > 0, jnp.log(count), NEVER).T


def parity():
    return lax.rem(lax.axis_index("mesh"), 2)


def start_body(once, twice, states, entering, all_gain, all_halo,
               far, own, gain, halo, normed, cross, inner, sems):
    lead = lax.axis_index("lead")
    small = ((all_gain, gain), (all_halo, halo))
    copies = [pltpu.make_async_copy(source, target, sems.at[i]) for i, (source, target) in enumerate(small)]
    for copy in copies:
        copy.start()
    choices = (
        (lead == once, entering, 1),
        (lead == twice, entering, 0),
        ((lead != once) & (lead != twice), states, 0),
    )
    for chosen, source, step in choices:

        @pl.when(chosen)
        def _(source=source, step=step):
            pltpu.make_async_copy(source.at[step, 1], own, sems.at[3]).start()
            pltpu.make_async_copy(source.at[step, 0], far, sems.at[4]).start()

    for copy in copies:
        copy.wait()
    odd = parity()
    edge = halo.shape[1]
    pltpu.make_async_copy(states.at[0, 1], own, sems.at[3]).wait()
    rows = normalised(own[...], gain[...])
    normed[...] = rows
    picked = picked_rows(rows, halo, odd)
    cross[:edge], inner[...] = picked[:edge], picked[edge:]
    pltpu.make_async_copy(states.at[0, 0], far, sems.at[4]).wait()
    low, high = halo[0:1], halo[1:2]
    cross[edge:] = rows_of(normalised(far[...], gain[...]), jnp.where(odd == 1, high, low))


def queries_of(rows, weight):
    return jnp.dot(rows, weight, preferred_element_type=F32).astype(BF) * BF(HEAD_DIM ** -0.5)


def stream_body(normed, wq, wk, wv, wo, q, vq, vk, vv, vo, sems):
    copies = []
    for i, (source, target) in enumerate(((wq, vq), (wk, vk), (wv, vv), (wo, vo))):
        depth = source.shape[0] // CHUNKS
        for j in range(CHUNKS):
            at = pl.ds(j * depth, depth)
            copies.append(pltpu.make_async_copy(source.at[at], target.at[at], sems.at[i, j]))
            copies[-1].start()
    for copy in copies[:CHUNKS]:
        copy.wait()
    q[...] = queries_of(normed[...], vq[...])
    for copy in copies[CHUNKS:]:
        copy.wait()


def project_first_body(normed, wq, senders, q, table):
    bias_table(senders, parity(), table)
    q[...] = queries_of(normed[...], wq[...])


def project_body(normed, wq, q):
    q[...] = queries_of(normed[...], wq[...])


def far_first_body(far, gain, halo, token, normed, inner):
    rows = normalised(far[...], gain[...])
    normed[...] = rows
    low, high = halo[0:1], halo[1:2]
    inner[...] = rows_of(rows, jnp.where(parity() == 1, low, high))


def attention(q, normed, cross, inner, table, wk, wv, attended):
    rows = jnp.concatenate([normed[...], cross, inner], axis=0)
    k = jnp.dot(rows, wk[...], preferred_element_type=F32).astype(BF)
    v = jnp.dot(rows, wv[...], preferred_element_type=F32).astype(BF)
    bias = table[...]
    nodes, width = q.shape
    bias = jnp.concatenate([bias, bias], axis=0)
    first = lax.broadcasted_iota(jnp.int32, (nodes, LANES), 1) < HEAD_DIM
    ones = jnp.ones((table.shape[1], LANES), BF)
    for i in range(width // LANES):
        at = slice(i * LANES, (i + 1) * LANES)
        pair = q[:, at]
        zero = jnp.zeros_like(pair)
        both = jnp.concatenate([jnp.where(first, pair, zero), jnp.where(first, zero, pair)], axis=0)
        scores = lax.dot_general(both, k[:, at], (((1,), (1,)), ((), ())), preferred_element_type=F32) + bias
        expo = jnp.exp(scores - jnp.max(scores, axis=1, keepdims=True)).astype(BF)
        sums = jnp.dot(expo, jnp.concatenate([v[:, at], ones], axis=1), preferred_element_type=F32)
        top = sums[:nodes, :LANES] / sums[:nodes, LANES:]
        low = sums[nodes:, :LANES] / sums[nodes:, LANES:]
        attended[:, at] = jnp.where(first, top, low).astype(BF)


def attend(state, q, normed, cross, inner, table, wk, wv, wo, attended):
    attention(q, normed, cross, inner, table, wk, wv, attended)
    update = jnp.dot(attended[...], wo[...], preferred_element_type=F32)
    return (state[...].astype(F32) + update).astype(BF)


def middle_body(splits, state, q, normed, cross, inner, table, wk, wv, wo, gain, halo,
                new_state, new_normed, new_cross, new_inner, *rest):
    edge = halo.shape[1]
    if splits:
        later, attended = rest
        later[...] = cross[edge:]
    else:
        attended, = rest
    moved = attend(state, q, normed, cross[:edge], inner[...], table, wk, wv, wo, attended)
    new_state[...] = moved
    rows = normalised(moved, gain[...])
    new_normed[...] = rows
    picked = picked_rows(rows, halo, parity())
    new_cross[...] = picked[:edge]
    new_inner[...] = picked[edge:]


def last_body(index, state, q, normed, cross, inner, table, wk, wv, wo, out, attended):
    special = lax.axis_index("lead") == index

    @pl.when(special)
    def _():
        out[...] = state[...]

    @pl.when(jnp.logical_not(special))
    def _():
        out[...] = attend(state, q, normed, cross[...], inner[...], table, wk, wv, wo, attended)


def finish_body(here, there, out, sems):
    copies = [pltpu.make_async_copy(x, out.at[0, i], sems.at[i]) for i, x in enumerate((here, there))]
    for copy in copies:
        copy.start()
    for copy in copies:
        copy.wait()


def per_device(states, entering, norm_gain, wq, wk, wv, wo, senders, halo_rows):
    leads, places = lax.axis_size("lead"), lax.axis_size("mesh")
    members, nodes, width = states.shape[1:]
    edge = halo_rows.shape[2]
    gain, halo, senders = norm_gain[None], halo_rows[0], senders.T
    states, entering = (pltpu.with_memory_space_constraint(x, pltpu.HBM) for x in (states, entering))
    vq, vk, vv, vo = wq, wk, wv, wo
    inner_route = [(i, i ^ 1) for i in range(places)]
    cross_route = [
        (a * places + i, ((a + leads // 2) % leads) * places + i if i in (0, places - 1) else a * places + ((i - 1) ^ 1) + 1)
        for a in range(leads)
        for i in range(places)
    ]
    route = [(i, (i + 2) % leads) for i in range(leads)]
    block, rim, rims = shape(nodes, width), shape(edge, width), shape(2 * edge, width)
    dma = pltpu.SemaphoreType.DMA

    def crossed(cross):
        return lax.ppermute(cross, ("lead", "mesh"), cross_route)

    def swapped(inner):
        return lax.ppermute(inner, "mesh", inner_route)

    def project(normed):
        return call(project_body, "project", [normed, vq], [VMEM] * 2, block, VMEM, micros=MP)

    def middle(name, splits, state, q, normed, cross, inner):
        return call(
            functools.partial(middle_body, splits), name,
            [state, q, normed, cross, inner, table, vk, vv, vo, gain, halo], [VMEM] * 11,
            [block, block, rim, rim] + [rim] * splits, [VMEM] * (4 + splits), [pltpu.VMEM((nodes, width), BF)],
        )

    def last(name, index, state, q, normed, cross, inner):
        return call(
            functools.partial(last_body, index), name,
            [state, q, normed, cross, inner, table, vk, vv, vo], [VMEM] * 9,
            block, VMEM, [pltpu.VMEM((nodes, width), BF)], micros=ML,
        )

    far, state1, gain, halo, normed1, cross, inner = call(
        functools.partial(start_body, leads - 2, leads - 1), "start",
        [states, entering] + [pltpu.with_memory_space_constraint(x, pltpu.HBM) for x in (gain, halo)],
        [HBM] * 4,
        [block, block] + [shape(*x.shape, dtype=x.dtype) for x in (gain, halo)] + [block, rims, rim],
        [VMEM] * 7, [dma((5,))], micros=MS,
    )
    cross = crossed(cross)
    inner = swapped(inner)
    q1, table = call(
        project_first_body, "project_first", [normed1, vq, senders], [VMEM] * 3,
        [block, shape(nodes, nodes + 2 * edge, dtype=F32)], [VMEM] * 2, micros=MP,
    )
    far = lax.ppermute(far, "lead", route)
    state1, normed1, cross1, inner1, halo0 = middle("middle_1", True, state1, q1, normed1, cross, inner)
    cross1 = crossed(cross1)
    inner1 = swapped(inner1)
    q1 = project(normed1)
    halo0 = lax.ppermute(halo0, "lead", route)
    near = last("last_1", leads - 2, state1, q1, normed1, cross1, inner1)
    arrived = lax.ppermute(near, "lead", route)
    normed0, inner0 = call(
        far_first_body, "far_first", [far, gain, halo, near], [VMEM] * 3 + [ANY], [block, rim], [VMEM] * 2,
    )
    inner0 = swapped(inner0)
    q0 = project(normed0)
    state0, normed0, cross0, inner0 = middle("middle_0", False, far, q0, normed0, halo0, inner0)
    cross0 = crossed(cross0)
    inner0 = swapped(inner0)
    q0 = project(normed0)
    here = last("last_0", 0, state0, q0, normed0, cross0, inner0)
    return call(
        finish_body, "finish", [here, arrived], [VMEM] * 2,
        shape(1, members, nodes, width), HBM, [dma((2,))],
    )


def solution(mesh):
    P = jax.sharding.PartitionSpec
    in_specs = (
        P("lead", None, "mesh", None),
        P(None, None, "mesh", None),
        P(),
        P(),
        P(),
        P(),
        P(),
        P("mesh", None),
        P("mesh", None, None),
    )
    return jax.shard_map(
        per_device, mesh=mesh, in_specs=in_specs, out_specs=P("lead", None, "mesh", None), check_vma=False
    )
```

```python
import functools

import jax
import jax.numpy as jnp
from jax import lax
from jax.experimental import pallas as pl
from jax.experimental.pallas import tpu as pltpu

HEAD_DIM = 64
LANES = 128
NEVER = -1e30
BF = jnp.bfloat16
F32 = jnp.float32
MS = 3.0
MP = 1.0
ML = 1.0
VMEM_BYTES = 16 * 1024 * 1024
VMEM = pl.BlockSpec(memory_space=pltpu.VMEM)
HBM = pl.BlockSpec(memory_space=pltpu.HBM)
ANY = pl.BlockSpec(memory_space=pl.ANY)


def shape(*dims, dtype=BF):
    return jax.ShapeDtypeStruct(dims, dtype)


def call(body, name, ins, specs, outs, out_specs, scratch=(), micros=1.0, **more):
    return pl.pallas_call(
        body,
        out_shape=outs,
        in_specs=specs,
        out_specs=out_specs,
        scratch_shapes=list(scratch),
        compiler_params=pltpu.CompilerParams(vmem_limit_bytes=VMEM_BYTES),
        cost_estimate=pl.CostEstimate(flops=int(micros * 1e9), bytes_accessed=1000, transcendentals=0),
        name=name,
        **more,
    )(*ins)


def normalised(x, gain):
    values = x.astype(F32)
    centred = values - jnp.mean(values, axis=-1, keepdims=True)
    spread = jnp.mean(centred * centred, axis=-1, keepdims=True)
    return (centred * lax.rsqrt(spread + 1e-05) * gain).astype(BF)


def rows_of(table, indices):
    spots = lax.broadcasted_iota(jnp.int32, (table.shape[0], indices.shape[1]), 0)
    picks = jnp.where(spots == indices, 1.0, 0.0)
    return jnp.dot(picks.T.astype(BF), table, preferred_element_type=F32).astype(BF)


def picked_rows(rows, halo, odd):
    low, high = halo[0:1], halo[1:2]
    first, second = jnp.where(odd == 1, high, low), jnp.where(odd == 1, low, high)
    return rows_of(rows, jnp.concatenate([first, second], axis=1))


def bias_table(senders, odd, table):
    nodes = table.shape[0]
    count = jnp.zeros((table.shape[1], nodes), F32)
    spots = lax.broadcasted_iota(jnp.int32, count.shape, 0)
    half = (table.shape[1] - nodes) // 2
    spots = jnp.where((spots >= nodes) & (odd == 1), jnp.where(spots >= nodes + half, spots - half, spots + half), spots)
    for j in range(senders.shape[0]):
        count += jnp.where(spots == senders[j:j + 1], 1.0, 0.0)
    table[...] = jnp.where(count > 0, jnp.log(count), NEVER).T


def parity():
    return lax.rem(lax.axis_index("mesh"), 2)


def start_body(once, twice, states, entering, all_gain, all_halo,
               far, own, gain, halo, normed, cross, inner, sems):
    lead = lax.axis_index("lead")
    small = ((all_gain, gain), (all_halo, halo))
    copies = [pltpu.make_async_copy(source, target, sems.at[i]) for i, (source, target) in enumerate(small)]
    for copy in copies:
        copy.start()
    choices = (
        (lead == once, entering, 1),
        (lead == twice, entering, 0),
        ((lead != once) & (lead != twice), states, 0),
    )
    for chosen, source, step in choices:

        @pl.when(chosen)
        def _(source=source, step=step):
            pltpu.make_async_copy(source.at[step, 1], own, sems.at[3]).start()
            pltpu.make_async_copy(source.at[step, 0], far, sems.at[4]).start()

    for copy in copies:
        copy.wait()
    odd = parity()
    edge = halo.shape[1]
    pltpu.make_async_copy(states.at[0, 1], own, sems.at[3]).wait()
    rows = normalised(own[...], gain[...])
    normed[...] = rows
    picked = picked_rows(rows, halo, odd)
    cross[:edge], inner[...] = picked[:edge], picked[edge:]
    pltpu.make_async_copy(states.at[0, 0], far, sems.at[4]).wait()
    low, high = halo[0:1], halo[1:2]
    cross[edge:] = rows_of(normalised(far[...], gain[...]), jnp.where(odd == 1, high, low))


def queries_of(rows, weight):
    return jnp.dot(rows, weight, preferred_element_type=F32).astype(BF) * BF(HEAD_DIM ** -0.5)


def stream_body(normed, wq, wk, wv, wo, q, vq, vk, vv, vo, sems):
    copies = []
    for i, (source, target) in enumerate(((wq, vq), (wk, vk), (wv, vv), (wo, vo))):
        depth = source.shape[0] // CHUNKS
        for j in range(CHUNKS):
            at = pl.ds(j * depth, depth)
            copies.append(pltpu.make_async_copy(source.at[at], target.at[at], sems.at[i, j]))
            copies[-1].start()
    for copy in copies[:CHUNKS]:
        copy.wait()
    q[...] = queries_of(normed[...], vq[...])
    for copy in copies[CHUNKS:]:
        copy.wait()


def project_first_body(normed, wq, senders, q, table):
    bias_table(senders, parity(), table)
    q[...] = queries_of(normed[...], wq[...])


def project_pass_body(normed, wq, inner, q, passed):
    passed[...] = inner[...]
    q[...] = queries_of(normed[...], wq[...])


def project_body(normed, wq, q):
    q[...] = queries_of(normed[...], wq[...])


def far_first_body(far, gain, halo, token, normed, inner):
    rows = normalised(far[...], gain[...])
    normed[...] = rows
    low, high = halo[0:1], halo[1:2]
    inner[...] = rows_of(rows, jnp.where(parity() == 1, low, high))


def attention(q, normed, cross, inner, table, wk, wv, attended):
    rows = jnp.concatenate([normed[...], cross, inner], axis=0)
    k = jnp.dot(rows, wk[...], preferred_element_type=F32).astype(BF)
    v = jnp.dot(rows, wv[...], preferred_element_type=F32).astype(BF)
    bias = table[...]
    nodes, width = q.shape
    bias = jnp.concatenate([bias, bias], axis=0)
    first = lax.broadcasted_iota(jnp.int32, (nodes, LANES), 1) < HEAD_DIM
    ones = jnp.ones((table.shape[1], LANES), BF)
    for i in range(width // LANES):
        at = slice(i * LANES, (i + 1) * LANES)
        pair = q[:, at]
        zero = jnp.zeros_like(pair)
        both = jnp.concatenate([jnp.where(first, pair, zero), jnp.where(first, zero, pair)], axis=0)
        scores = lax.dot_general(both, k[:, at], (((1,), (1,)), ((), ())), preferred_element_type=F32) + bias
        expo = jnp.exp(scores - jnp.max(scores, axis=1, keepdims=True)).astype(BF)
        sums = jnp.dot(expo, jnp.concatenate([v[:, at], ones], axis=1), preferred_element_type=F32)
        top = sums[:nodes, :LANES] / sums[:nodes, LANES:]
        low = sums[nodes:, :LANES] / sums[nodes:, LANES:]
        attended[:, at] = jnp.where(first, top, low).astype(BF)


def attend(state, q, normed, cross, inner, table, wk, wv, wo, attended):
    attention(q, normed, cross, inner, table, wk, wv, attended)
    update = jnp.dot(attended[...], wo[...], preferred_element_type=F32)
    return (state[...].astype(F32) + update).astype(BF)


def middle_body(splits, state, q, normed, cross, inner, table, wk, wv, wo, gain, halo,
                new_state, new_normed, new_cross, new_inner, *rest):
    edge = halo.shape[1]
    if splits:
        later, attended = rest
        later[...] = cross[edge:]
    else:
        attended, = rest
    moved = attend(state, q, normed, cross[:edge], inner[...], table, wk, wv, wo, attended)
    new_state[...] = moved
    rows = normalised(moved, gain[...])
    new_normed[...] = rows
    picked = picked_rows(rows, halo, parity())
    new_cross[...] = picked[:edge]
    new_inner[...] = picked[edge:]


def last_body(index, state, q, normed, cross, inner, table, wk, wv, wo, out, attended):
    special = lax.axis_index("lead") == index

    @pl.when(special)
    def _():
        out[...] = state[...]

    @pl.when(jnp.logical_not(special))
    def _():
        out[...] = attend(state, q, normed, cross[...], inner[...], table, wk, wv, wo, attended)


def finish_body(here, there, out, sems):
    copies = [pltpu.make_async_copy(x, out.at[0, i], sems.at[i]) for i, x in enumerate((here, there))]
    for copy in copies:
        copy.start()
    for copy in copies:
        copy.wait()


def per_device(states, entering, norm_gain, wq, wk, wv, wo, senders, halo_rows):
    leads, places = lax.axis_size("lead"), lax.axis_size("mesh")
    members, nodes, width = states.shape[1:]
    edge = halo_rows.shape[2]
    gain, halo, senders = norm_gain[None], halo_rows[0], senders.T
    states, entering = (pltpu.with_memory_space_constraint(x, pltpu.HBM) for x in (states, entering))
    vq, vk, vv, vo = wq, wk, wv, wo
    inner_route = [(i, i ^ 1) for i in range(places)]
    cross_route = [
        (a * places + i, ((a + leads // 2) % leads) * places + i if i in (0, places - 1) else a * places + ((i - 1) ^ 1) + 1)
        for a in range(leads)
        for i in range(places)
    ]
    route = [(i, (i + 2) % leads) for i in range(leads)]
    block, rim, rims = shape(nodes, width), shape(edge, width), shape(2 * edge, width)
    dma = pltpu.SemaphoreType.DMA

    def crossed(cross):
        return lax.ppermute(cross, ("lead", "mesh"), cross_route)

    def swapped(inner):
        return lax.ppermute(inner, "mesh", inner_route)

    def project(normed):
        return call(project_body, "project", [normed, vq], [VMEM] * 2, block, VMEM, micros=MP)

    def project_pass(normed, inner):
        return call(
            project_pass_body, "project", [normed, vq, inner], [VMEM] * 3, [block, rim], [VMEM] * 2, micros=MP,
        )

    def middle(name, splits, state, q, normed, cross, inner):
        return call(
            functools.partial(middle_body, splits), name,
            [state, q, normed, cross, inner, table, vk, vv, vo, gain, halo], [VMEM] * 11,
            [block, block, rim, rim] + [rim] * splits, [VMEM] * (4 + splits), [pltpu.VMEM((nodes, width), BF)],
        )

    def last(name, index, state, q, normed, cross, inner):
        return call(
            functools.partial(last_body, index), name,
            [state, q, normed, cross, inner, table, vk, vv, vo], [VMEM] * 9,
            block, VMEM, [pltpu.VMEM((nodes, width), BF)], micros=ML,
        )

    far, state1, gain, halo, normed1, cross, inner = call(
        functools.partial(start_body, leads - 2, leads - 1), "start",
        [states, entering] + [pltpu.with_memory_space_constraint(x, pltpu.HBM) for x in (gain, halo)],
        [HBM] * 4,
        [block, block] + [shape(*x.shape, dtype=x.dtype) for x in (gain, halo)] + [block, rims, rim],
        [VMEM] * 7, [dma((5,))], micros=MS,
    )
    cross = crossed(cross)
    inner = swapped(inner)
    q1, table = call(
        project_first_body, "project_first", [normed1, vq, senders], [VMEM] * 3,
        [block, shape(nodes, nodes + 2 * edge, dtype=F32)], [VMEM] * 2, micros=MP,
    )
    far = lax.ppermute(far, "lead", route)
    state1, normed1, cross1, inner1, halo0 = middle("middle_1", True, state1, q1, normed1, cross, inner)
    cross1 = crossed(cross1)
    inner1 = swapped(inner1)
    q1, halo0 = project_pass(normed1, halo0)
    halo0 = lax.ppermute(halo0, "lead", route)
    near = last("last_1", leads - 2, state1, q1, normed1, cross1, inner1)
    arrived = lax.ppermute(near, "lead", route)
    normed0, inner0 = call(
        far_first_body, "far_first", [far, gain, halo, near], [VMEM] * 3 + [ANY], [block, rim], [VMEM] * 2,
    )
    inner0 = swapped(inner0)
    q0 = project(normed0)
    state0, normed0, cross0, inner0 = middle("middle_0", False, far, q0, normed0, halo0, inner0)
    cross0 = crossed(cross0)
    inner0 = swapped(inner0)
    q0 = project(normed0)
    here = last("last_0", 0, state0, q0, normed0, cross0, inner0)
    return call(
        finish_body, "finish", [here, arrived], [VMEM] * 2,
        shape(1, members, nodes, width), HBM, [dma((2,))],
    )


def solution(mesh):
    P = jax.sharding.PartitionSpec
    in_specs = (
        P("lead", None, "mesh", None),
        P(None, None, "mesh", None),
        P(),
        P(),
        P(),
        P(),
        P(),
        P("mesh", None),
        P("mesh", None, None),
    )
    return jax.shard_map(
        per_device, mesh=mesh, in_specs=in_specs, out_specs=P("lead", None, "mesh", None), check_vma=False
    )
```

```python
import functools

import jax
import jax.numpy as jnp
from jax import lax
from jax.experimental import pallas as pl
from jax.experimental.pallas import tpu as pltpu

HEAD_DIM = 64
LANES = 128
BF = jnp.bfloat16
F32 = jnp.float32
MS = 3.0
MP = 1.0
ML = 1.0
VMEM_BYTES = 16 * 1024 * 1024
VMEM = pl.BlockSpec(memory_space=pltpu.VMEM)
HBM = pl.BlockSpec(memory_space=pltpu.HBM)
ANY = pl.BlockSpec(memory_space=pl.ANY)


def shape(*dims, dtype=BF):
    return jax.ShapeDtypeStruct(dims, dtype)


def call(body, name, ins, specs, outs, out_specs, scratch=(), micros=1.0, **more):
    return pl.pallas_call(
        body,
        out_shape=outs,
        in_specs=specs,
        out_specs=out_specs,
        scratch_shapes=list(scratch),
        compiler_params=pltpu.CompilerParams(vmem_limit_bytes=VMEM_BYTES),
        cost_estimate=pl.CostEstimate(flops=int(micros * 1e9), bytes_accessed=1000, transcendentals=0),
        name=name,
        **more,
    )(*ins)


def normalised(x, gain):
    values = x.astype(F32)
    centred = values - jnp.mean(values, axis=-1, keepdims=True)
    spread = jnp.mean(centred * centred, axis=-1, keepdims=True)
    return (centred * lax.rsqrt(spread + 1e-05) * gain).astype(BF)


def rows_of(table, indices):
    spots = lax.broadcasted_iota(jnp.int32, (table.shape[0], indices.shape[1]), 0)
    picks = jnp.where(spots == indices, 1.0, 0.0)
    return jnp.dot(picks.T.astype(BF), table, preferred_element_type=F32).astype(BF)


def picked_rows(rows, halo, odd):
    low, high = halo[0:1], halo[1:2]
    first, second = jnp.where(odd == 1, high, low), jnp.where(odd == 1, low, high)
    return rows_of(rows, jnp.concatenate([first, second], axis=1))


def count_table(senders, odd, table):
    nodes = table.shape[0]
    count = jnp.zeros((table.shape[1], nodes), F32)
    spots = lax.broadcasted_iota(jnp.int32, count.shape, 0)
    half = (table.shape[1] - nodes) // 2
    spots = jnp.where((spots >= nodes) & (odd == 1), jnp.where(spots >= nodes + half, spots - half, spots + half), spots)
    for j in range(senders.shape[0]):
        count += jnp.where(spots == senders[j:j + 1], 1.0, 0.0)
    table[...] = count.T


def parity():
    return lax.rem(lax.axis_index("mesh"), 2)


def start_body(once, twice, states, entering, all_gain, all_halo,
               far, own, gain, halo, normed, cross, inner, sems):
    lead = lax.axis_index("lead")
    small = ((all_gain, gain), (all_halo, halo))
    copies = [pltpu.make_async_copy(source, target, sems.at[i]) for i, (source, target) in enumerate(small)]
    for copy in copies:
        copy.start()
    choices = (
        (lead == once, entering, 1),
        (lead == twice, entering, 0),
        ((lead != once) & (lead != twice), states, 0),
    )
    for chosen, source, step in choices:

        @pl.when(chosen)
        def _(source=source, step=step):
            pltpu.make_async_copy(source.at[step, 1], own, sems.at[3]).start()
            pltpu.make_async_copy(source.at[step, 0], far, sems.at[4]).start()

    for copy in copies:
        copy.wait()
    odd = parity()
    edge = halo.shape[1]
    pltpu.make_async_copy(states.at[0, 1], own, sems.at[3]).wait()
    rows = normalised(own[...], gain[...])
    normed[...] = rows
    picked = picked_rows(rows, halo, odd)
    cross[:edge], inner[...] = picked[:edge], picked[edge:]
    pltpu.make_async_copy(states.at[0, 0], far, sems.at[4]).wait()
    low, high = halo[0:1], halo[1:2]
    cross[edge:] = rows_of(normalised(far[...], gain[...]), jnp.where(odd == 1, high, low))


def queries_of(rows, weight):
    return jnp.dot(rows, weight, preferred_element_type=F32).astype(BF) * BF(HEAD_DIM ** -0.5)


def stream_body(normed, wq, wk, wv, wo, q, vq, vk, vv, vo, sems):
    copies = []
    for i, (source, target) in enumerate(((wq, vq), (wk, vk), (wv, vv), (wo, vo))):
        depth = source.shape[0] // CHUNKS
        for j in range(CHUNKS):
            at = pl.ds(j * depth, depth)
            copies.append(pltpu.make_async_copy(source.at[at], target.at[at], sems.at[i, j]))
            copies[-1].start()
    for copy in copies[:CHUNKS]:
        copy.wait()
    q[...] = queries_of(normed[...], vq[...])
    for copy in copies[CHUNKS:]:
        copy.wait()


def project_first_body(normed, wq, senders, q, table):
    count_table(senders, parity(), table)
    q[...] = queries_of(normed[...], wq[...])


def project_pass_body(normed, wq, inner, q, passed):
    passed[...] = inner[...]
    q[...] = queries_of(normed[...], wq[...])


def project_body(normed, wq, q):
    q[...] = queries_of(normed[...], wq[...])


def far_first_body(far, gain, halo, token, normed, inner):
    rows = normalised(far[...], gain[...])
    normed[...] = rows
    low, high = halo[0:1], halo[1:2]
    inner[...] = rows_of(rows, jnp.where(parity() == 1, low, high))


def attention(q, normed, cross, inner, table, wk, wv, attended):
    rows = jnp.concatenate([normed[...], cross, inner], axis=0)
    k = jnp.dot(rows, wk[...], preferred_element_type=F32).astype(BF)
    v = jnp.dot(rows, wv[...], preferred_element_type=F32).astype(BF)
    count = table[...]
    nodes, width = q.shape
    count = jnp.concatenate([count, count], axis=0)
    named = count > 0
    first = lax.broadcasted_iota(jnp.int32, (nodes, LANES), 1) < HEAD_DIM
    ones = jnp.ones((table.shape[1], LANES), BF)
    for i in range(width // LANES):
        at = slice(i * LANES, (i + 1) * LANES)
        pair = q[:, at]
        zero = jnp.zeros_like(pair)
        both = jnp.concatenate([jnp.where(first, pair, zero), jnp.where(first, zero, pair)], axis=0)
        scores = lax.dot_general(both, k[:, at], (((1,), (1,)), ((), ())), preferred_element_type=F32)
        scores = jnp.where(named, scores, -jnp.inf)
        expo = (jnp.exp(scores - jnp.max(scores, axis=1, keepdims=True)) * count).astype(BF)
        sums = jnp.dot(expo, jnp.concatenate([v[:, at], ones], axis=1), preferred_element_type=F32)
        top = sums[:nodes, :LANES] / sums[:nodes, LANES:]
        low = sums[nodes:, :LANES] / sums[nodes:, LANES:]
        attended[:, at] = jnp.where(first, top, low).astype(BF)


def attend(state, q, normed, cross, inner, table, wk, wv, wo, attended):
    attention(q, normed, cross, inner, table, wk, wv, attended)
    update = jnp.dot(attended[...], wo[...], preferred_element_type=F32)
    return (state[...].astype(F32) + update).astype(BF)


def middle_body(splits, state, q, normed, cross, inner, table, wk, wv, wo, gain, halo,
                new_state, new_normed, new_cross, new_inner, *rest):
    edge = halo.shape[1]
    if splits:
        later, attended = rest
        later[...] = cross[edge:]
    else:
        attended, = rest
    moved = attend(state, q, normed, cross[:edge], inner[...], table, wk, wv, wo, attended)
    new_state[...] = moved
    rows = normalised(moved, gain[...])
    new_normed[...] = rows
    picked = picked_rows(rows, halo, parity())
    new_cross[...] = picked[:edge]
    new_inner[...] = picked[edge:]


def last_body(index, state, q, normed, cross, inner, table, wk, wv, wo, out, attended):
    special = lax.axis_index("lead") == index

    @pl.when(special)
    def _():
        out[...] = state[...]

    @pl.when(jnp.logical_not(special))
    def _():
        out[...] = attend(state, q, normed, cross[...], inner[...], table, wk, wv, wo, attended)


def finish_body(here, there, out, sems):
    copies = [pltpu.make_async_copy(x, out.at[0, i], sems.at[i]) for i, x in enumerate((here, there))]
    for copy in copies:
        copy.start()
    for copy in copies:
        copy.wait()


def per_device(states, entering, norm_gain, wq, wk, wv, wo, senders, halo_rows):
    leads, places = lax.axis_size("lead"), lax.axis_size("mesh")
    members, nodes, width = states.shape[1:]
    edge = halo_rows.shape[2]
    gain, halo, senders = norm_gain[None], halo_rows[0], senders.T
    states, entering = (pltpu.with_memory_space_constraint(x, pltpu.HBM) for x in (states, entering))
    vq, vk, vv, vo = wq, wk, wv, wo
    inner_route = [(i, i ^ 1) for i in range(places)]
    cross_route = [
        (a * places + i, ((a + leads // 2) % leads) * places + i if i in (0, places - 1) else a * places + ((i - 1) ^ 1) + 1)
        for a in range(leads)
        for i in range(places)
    ]
    route = [(i, (i + 2) % leads) for i in range(leads)]
    block, rim, rims = shape(nodes, width), shape(edge, width), shape(2 * edge, width)
    dma = pltpu.SemaphoreType.DMA

    def crossed(cross):
        return lax.ppermute(cross, ("lead", "mesh"), cross_route)

    def swapped(inner):
        return lax.ppermute(inner, "mesh", inner_route)

    def project(normed):
        return call(project_body, "project", [normed, vq], [VMEM] * 2, block, VMEM, micros=MP)

    def project_pass(normed, inner):
        return call(
            project_pass_body, "project", [normed, vq, inner], [VMEM] * 3, [block, rim], [VMEM] * 2, micros=MP,
        )

    def middle(name, splits, state, q, normed, cross, inner):
        return call(
            functools.partial(middle_body, splits), name,
            [state, q, normed, cross, inner, table, vk, vv, vo, gain, halo], [VMEM] * 11,
            [block, block, rim, rim] + [rim] * splits, [VMEM] * (4 + splits), [pltpu.VMEM((nodes, width), BF)],
        )

    def last(name, index, state, q, normed, cross, inner):
        return call(
            functools.partial(last_body, index), name,
            [state, q, normed, cross, inner, table, vk, vv, vo], [VMEM] * 9,
            block, VMEM, [pltpu.VMEM((nodes, width), BF)], micros=ML,
        )

    far, state1, gain, halo, normed1, cross, inner = call(
        functools.partial(start_body, leads - 2, leads - 1), "start",
        [states, entering] + [pltpu.with_memory_space_constraint(x, pltpu.HBM) for x in (gain, halo)],
        [HBM] * 4,
        [block, block] + [shape(*x.shape, dtype=x.dtype) for x in (gain, halo)] + [block, rims, rim],
        [VMEM] * 7, [dma((5,))], micros=MS,
    )
    cross = crossed(cross)
    inner = swapped(inner)
    q1, table = call(
        project_first_body, "project_first", [normed1, vq, senders], [VMEM] * 3,
        [block, shape(nodes, nodes + 2 * edge, dtype=F32)], [VMEM] * 2, micros=MP,
    )
    far = lax.ppermute(far, "lead", route)
    state1, normed1, cross1, inner1, halo0 = middle("middle_1", True, state1, q1, normed1, cross, inner)
    cross1 = crossed(cross1)
    inner1 = swapped(inner1)
    q1, halo0 = project_pass(normed1, halo0)
    halo0 = lax.ppermute(halo0, "lead", route)
    near = last("last_1", leads - 2, state1, q1, normed1, cross1, inner1)
    arrived = lax.ppermute(near, "lead", route)
    normed0, inner0 = call(
        far_first_body, "far_first", [far, gain, halo, near], [VMEM] * 3 + [ANY], [block, rim], [VMEM] * 2,
    )
    inner0 = swapped(inner0)
    q0 = project(normed0)
    state0, normed0, cross0, inner0 = middle("middle_0", False, far, q0, normed0, halo0, inner0)
    cross0 = crossed(cross0)
    inner0 = swapped(inner0)
    q0 = project(normed0)
    here = last("last_0", 0, state0, q0, normed0, cross0, inner0)
    return call(
        finish_body, "finish", [here, arrived], [VMEM] * 2,
        shape(1, members, nodes, width), HBM, [dma((2,))],
    )


def solution(mesh):
    P = jax.sharding.PartitionSpec
    in_specs = (
        P("lead", None, "mesh", None),
        P(None, None, "mesh", None),
        P(),
        P(),
        P(),
        P(),
        P(),
        P("mesh", None),
        P("mesh", None, None),
    )
    return jax.shard_map(
        per_device, mesh=mesh, in_specs=in_specs, out_specs=P("lead", None, "mesh", None), check_vma=False
    )
```

```python
import functools

import jax
import jax.numpy as jnp
from jax import lax
from jax.experimental import pallas as pl
from jax.experimental.pallas import tpu as pltpu

HEAD_DIM = 64
LANES = 128
NEVER = -jnp.inf
BF = jnp.bfloat16
F32 = jnp.float32
MS = 3.0
MP = 1.0
ML = 1.0
VMEM_BYTES = 16 * 1024 * 1024
VMEM = pl.BlockSpec(memory_space=pltpu.VMEM)
HBM = pl.BlockSpec(memory_space=pltpu.HBM)
ANY = pl.BlockSpec(memory_space=pl.ANY)


def shape(*dims, dtype=BF):
    return jax.ShapeDtypeStruct(dims, dtype)


def call(body, name, ins, specs, outs, out_specs, scratch=(), micros=1.0, **more):
    return pl.pallas_call(
        body,
        out_shape=outs,
        in_specs=specs,
        out_specs=out_specs,
        scratch_shapes=list(scratch),
        compiler_params=pltpu.CompilerParams(vmem_limit_bytes=VMEM_BYTES),
        cost_estimate=pl.CostEstimate(flops=int(micros * 1e9), bytes_accessed=1000, transcendentals=0),
        name=name,
        **more,
    )(*ins)


def normalised(x, gain):
    values = x.astype(F32)
    centred = values - jnp.mean(values, axis=-1, keepdims=True)
    spread = jnp.mean(centred * centred, axis=-1, keepdims=True)
    return (centred * lax.rsqrt(spread + 1e-05) * gain).astype(BF)


def rows_of(table, indices):
    spots = lax.broadcasted_iota(jnp.int32, (table.shape[0], indices.shape[1]), 0)
    picks = jnp.where(spots == indices, 1.0, 0.0)
    return jnp.dot(picks.T.astype(BF), table, preferred_element_type=F32).astype(BF)


def picked_rows(rows, halo, odd):
    low, high = halo[0:1], halo[1:2]
    first, second = jnp.where(odd == 1, high, low), jnp.where(odd == 1, low, high)
    return rows_of(rows, jnp.concatenate([first, second], axis=1))


def bias_table(senders, odd, table):
    nodes = table.shape[0]
    count = jnp.zeros((table.shape[1], nodes), F32)
    spots = lax.broadcasted_iota(jnp.int32, count.shape, 0)
    half = (table.shape[1] - nodes) // 2
    spots = jnp.where((spots >= nodes) & (odd == 1), jnp.where(spots >= nodes + half, spots - half, spots + half), spots)
    for j in range(senders.shape[0]):
        count += jnp.where(spots == senders[j:j + 1], 1.0, 0.0)
    table[...] = jnp.where(count > 0, jnp.log(count), NEVER).T


def parity():
    return lax.rem(lax.axis_index("mesh"), 2)


def start_body(once, twice, states, entering, all_gain, all_halo,
               far, own, gain, halo, normed, cross, inner, sems):
    lead = lax.axis_index("lead")
    small = ((all_gain, gain), (all_halo, halo))
    copies = [pltpu.make_async_copy(source, target, sems.at[i]) for i, (source, target) in enumerate(small)]
    for copy in copies:
        copy.start()
    choices = (
        (lead == once, entering, 1),
        (lead == twice, entering, 0),
        ((lead != once) & (lead != twice), states, 0),
    )
    for chosen, source, step in choices:

        @pl.when(chosen)
        def _(source=source, step=step):
            pltpu.make_async_copy(source.at[step, 1], own, sems.at[3]).start()
            pltpu.make_async_copy(source.at[step, 0], far, sems.at[4]).start()

    for copy in copies:
        copy.wait()
    odd = parity()
    edge = halo.shape[1]
    pltpu.make_async_copy(states.at[0, 1], own, sems.at[3]).wait()
    rows = normalised(own[...], gain[...])
    normed[...] = rows
    picked = picked_rows(rows, halo, odd)
    cross[:edge], inner[...] = picked[:edge], picked[edge:]
    pltpu.make_async_copy(states.at[0, 0], far, sems.at[4]).wait()
    low, high = halo[0:1], halo[1:2]
    cross[edge:] = rows_of(normalised(far[...], gain[...]), jnp.where(odd == 1, high, low))


def queries_of(rows, weight):
    return jnp.dot(rows, weight, preferred_element_type=F32).astype(BF) * BF(HEAD_DIM ** -0.5)


def stream_body(normed, wq, wk, wv, wo, q, vq, vk, vv, vo, sems):
    copies = []
    for i, (source, target) in enumerate(((wq, vq), (wk, vk), (wv, vv), (wo, vo))):
        depth = source.shape[0] // CHUNKS
        for j in range(CHUNKS):
            at = pl.ds(j * depth, depth)
            copies.append(pltpu.make_async_copy(source.at[at], target.at[at], sems.at[i, j]))
            copies[-1].start()
    for copy in copies[:CHUNKS]:
        copy.wait()
    q[...] = queries_of(normed[...], vq[...])
    for copy in copies[CHUNKS:]:
        copy.wait()


def project_first_body(normed, wq, senders, q, table):
    bias_table(senders, parity(), table)
    q[...] = queries_of(normed[...], wq[...])


def project_pass_body(normed, wq, inner, q, passed):
    passed[...] = inner[...]
    q[...] = queries_of(normed[...], wq[...])


def project_body(normed, wq, q):
    q[...] = queries_of(normed[...], wq[...])


def far_first_body(far, gain, halo, token, normed, inner):
    rows = normalised(far[...], gain[...])
    normed[...] = rows
    low, high = halo[0:1], halo[1:2]
    inner[...] = rows_of(rows, jnp.where(parity() == 1, low, high))


def attention(q, normed, cross, inner, table, wk, wv, attended):
    rows = jnp.concatenate([normed[...], cross, inner], axis=0)
    k = jnp.dot(rows, wk[...], preferred_element_type=F32).astype(BF)
    v = jnp.dot(rows, wv[...], preferred_element_type=F32).astype(BF)
    bias = table[...]
    nodes, width = q.shape
    bias = jnp.concatenate([bias, bias], axis=0)
    first = lax.broadcasted_iota(jnp.int32, (nodes, LANES), 1) < HEAD_DIM
    ones = jnp.ones((table.shape[1], LANES), BF)
    for i in range(width // LANES):
        at = slice(i * LANES, (i + 1) * LANES)
        pair = q[:, at]
        zero = jnp.zeros_like(pair)
        both = jnp.concatenate([jnp.where(first, pair, zero), jnp.where(first, zero, pair)], axis=0)
        scores = lax.dot_general(both, k[:, at], (((1,), (1,)), ((), ())), preferred_element_type=F32) + bias
        expo = jnp.exp(scores - jnp.max(scores, axis=1, keepdims=True)).astype(BF)
        sums = jnp.dot(expo, jnp.concatenate([v[:, at], ones], axis=1), preferred_element_type=F32)
        top = sums[:nodes, :LANES] / sums[:nodes, LANES:]
        low = sums[nodes:, :LANES] / sums[nodes:, LANES:]
        attended[:, at] = jnp.where(first, top, low).astype(BF)


def attend(state, q, normed, cross, inner, table, wk, wv, wo, attended):
    attention(q, normed, cross, inner, table, wk, wv, attended)
    update = jnp.dot(attended[...], wo[...], preferred_element_type=F32)
    return (state[...].astype(F32) + update).astype(BF)


def middle_body(splits, state, q, normed, cross, inner, table, wk, wv, wo, gain, halo,
                new_state, new_normed, new_cross, new_inner, *rest):
    edge = halo.shape[1]
    if splits:
        later, attended = rest
        later[...] = cross[edge:]
    else:
        attended, = rest
    moved = attend(state, q, normed, cross[:edge], inner[...], table, wk, wv, wo, attended)
    new_state[...] = moved
    rows = normalised(moved, gain[...])
    new_normed[...] = rows
    picked = picked_rows(rows, halo, parity())
    new_cross[...] = picked[:edge]
    new_inner[...] = picked[edge:]


def last_body(index, state, q, normed, cross, inner, table, wk, wv, wo, out, attended):
    special = lax.axis_index("lead") == index

    @pl.when(special)
    def _():
        out[...] = state[...]

    @pl.when(jnp.logical_not(special))
    def _():
        out[...] = attend(state, q, normed, cross[...], inner[...], table, wk, wv, wo, attended)


def finish_body(here, there, out, sems):
    copies = [pltpu.make_async_copy(x, out.at[0, i], sems.at[i]) for i, x in enumerate((here, there))]
    for copy in copies:
        copy.start()
    for copy in copies:
        copy.wait()


def per_device(states, entering, norm_gain, wq, wk, wv, wo, senders, halo_rows):
    leads, places = lax.axis_size("lead"), lax.axis_size("mesh")
    members, nodes, width = states.shape[1:]
    edge = halo_rows.shape[2]
    gain, halo, senders = norm_gain[None], halo_rows[0], senders.T
    states, entering = (pltpu.with_memory_space_constraint(x, pltpu.HBM) for x in (states, entering))
    vq, vk, vv, vo = wq, wk, wv, wo
    inner_route = [(i, i ^ 1) for i in range(places)]
    cross_route = [
        (a * places + i, ((a + leads // 2) % leads) * places + i if i in (0, places - 1) else a * places + ((i - 1) ^ 1) + 1)
        for a in range(leads)
        for i in range(places)
    ]
    route = [(i, (i + 2) % leads) for i in range(leads)]
    block, rim, rims = shape(nodes, width), shape(edge, width), shape(2 * edge, width)
    dma = pltpu.SemaphoreType.DMA

    def crossed(cross):
        return lax.ppermute(cross, ("lead", "mesh"), cross_route)

    def swapped(inner):
        return lax.ppermute(inner, "mesh", inner_route)

    def project(normed):
        return call(project_body, "project", [normed, vq], [VMEM] * 2, block, VMEM, micros=MP)

    def project_pass(normed, inner):
        return call(
            project_pass_body, "project", [normed, vq, inner], [VMEM] * 3, [block, rim], [VMEM] * 2, micros=MP,
        )

    def middle(name, splits, state, q, normed, cross, inner):
        return call(
            functools.partial(middle_body, splits), name,
            [state, q, normed, cross, inner, table, vk, vv, vo, gain, halo], [VMEM] * 11,
            [block, block, rim, rim] + [rim] * splits, [VMEM] * (4 + splits), [pltpu.VMEM((nodes, width), BF)],
        )

    def last(name, index, state, q, normed, cross, inner):
        return call(
            functools.partial(last_body, index), name,
            [state, q, normed, cross, inner, table, vk, vv, vo], [VMEM] * 9,
            block, VMEM, [pltpu.VMEM((nodes, width), BF)], micros=ML,
        )

    far, state1, gain, halo, normed1, cross, inner = call(
        functools.partial(start_body, leads - 2, leads - 1), "start",
        [states, entering] + [pltpu.with_memory_space_constraint(x, pltpu.HBM) for x in (gain, halo)],
        [HBM] * 4,
        [block, block] + [shape(*x.shape, dtype=x.dtype) for x in (gain, halo)] + [block, rims, rim],
        [VMEM] * 7, [dma((5,))], micros=MS,
    )
    cross = crossed(cross)
    inner = swapped(inner)
    q1, table = call(
        project_first_body, "project_first", [normed1, vq, senders], [VMEM] * 3,
        [block, shape(nodes, nodes + 2 * edge, dtype=F32)], [VMEM] * 2, micros=MP,
    )
    far = lax.ppermute(far, "lead", route)
    state1, normed1, cross1, inner1, halo0 = middle("middle_1", True, state1, q1, normed1, cross, inner)
    cross1 = crossed(cross1)
    inner1 = swapped(inner1)
    q1, halo0 = project_pass(normed1, halo0)
    halo0 = lax.ppermute(halo0, "lead", route)
    near = last("last_1", leads - 2, state1, q1, normed1, cross1, inner1)
    arrived = lax.ppermute(near, "lead", route)
    normed0, inner0 = call(
        far_first_body, "far_first", [far, gain, halo, near], [VMEM] * 3 + [ANY], [block, rim], [VMEM] * 2,
    )
    inner0 = swapped(inner0)
    q0 = project(normed0)
    state0, normed0, cross0, inner0 = middle("middle_0", False, far, q0, normed0, halo0, inner0)
    cross0 = crossed(cross0)
    inner0 = swapped(inner0)
    q0 = project(normed0)
    here = last("last_0", 0, state0, q0, normed0, cross0, inner0)
    return call(
        finish_body, "finish", [here, arrived], [VMEM] * 2,
        shape(1, members, nodes, width), HBM, [dma((2,))],
    )


def solution(mesh):
    P = jax.sharding.PartitionSpec
    in_specs = (
        P("lead", None, "mesh", None),
        P(None, None, "mesh", None),
        P(),
        P(),
        P(),
        P(),
        P(),
        P("mesh", None),
        P("mesh", None, None),
    )
    return jax.shard_map(
        per_device, mesh=mesh, in_specs=in_specs, out_specs=P("lead", None, "mesh", None), check_vma=False
    )
```

```python
import functools

import jax
import jax.numpy as jnp
from jax import lax
from jax.experimental import pallas as pl
from jax.experimental.pallas import tpu as pltpu

HEAD_DIM = 64
LANES = 128
NEVER = -jnp.inf
BF = jnp.bfloat16
F32 = jnp.float32
MS = 3.0
MP = 1.0
ML = 1.0
VMEM_BYTES = 16 * 1024 * 1024
VMEM = pl.BlockSpec(memory_space=pltpu.VMEM)
HBM = pl.BlockSpec(memory_space=pltpu.HBM)
ANY = pl.BlockSpec(memory_space=pl.ANY)


def shape(*dims, dtype=BF):
    return jax.ShapeDtypeStruct(dims, dtype)


def call(body, name, ins, specs, outs, out_specs, scratch=(), micros=1.0, **more):
    return pl.pallas_call(
        body,
        out_shape=outs,
        in_specs=specs,
        out_specs=out_specs,
        scratch_shapes=list(scratch),
        compiler_params=pltpu.CompilerParams(vmem_limit_bytes=VMEM_BYTES),
        cost_estimate=pl.CostEstimate(flops=int(micros * 1e9), bytes_accessed=1000, transcendentals=0),
        name=name,
        **more,
    )(*ins)


def normalised(x, gain):
    values = x.astype(F32)
    centred = values - jnp.mean(values, axis=-1, keepdims=True)
    spread = jnp.mean(centred * centred, axis=-1, keepdims=True)
    return (centred * lax.rsqrt(spread + 1e-05) * gain).astype(BF)


def rows_of(table, indices):
    spots = lax.broadcasted_iota(jnp.int32, (table.shape[0], indices.shape[1]), 0)
    picks = jnp.where(spots == indices, 1.0, 0.0)
    return jnp.dot(picks.T.astype(BF), table, preferred_element_type=F32).astype(BF)


def picked_rows(rows, halo, odd):
    low, high = halo[0:1], halo[1:2]
    first, second = jnp.where(odd == 1, high, low), jnp.where(odd == 1, low, high)
    return rows_of(rows, jnp.concatenate([first, second], axis=1))


def bias_table(senders, odd, table):
    nodes = table.shape[0]
    count = jnp.zeros((table.shape[1], nodes), F32)
    spots = lax.broadcasted_iota(jnp.int32, count.shape, 0)
    half = (table.shape[1] - nodes) // 2
    spots = jnp.where((spots >= nodes) & (odd == 1), jnp.where(spots >= nodes + half, spots - half, spots + half), spots)
    for j in range(senders.shape[0]):
        count += jnp.where(spots == senders[j:j + 1], 1.0, 0.0)
    table[...] = jnp.where(count > 0, jnp.log(count), NEVER).T


def parity():
    return lax.rem(lax.axis_index("mesh"), 2)


def start_body(once, twice, states, entering, all_gain, all_halo,
               far, own, gain, halo, normed, cross, inner, sems):
    lead = lax.axis_index("lead")
    small = ((all_gain, gain), (all_halo, halo))
    copies = [pltpu.make_async_copy(source, target, sems.at[i]) for i, (source, target) in enumerate(small)]
    for copy in copies:
        copy.start()
    choices = (
        (lead == once, entering, 1),
        (lead == twice, entering, 0),
        ((lead != once) & (lead != twice), states, 0),
    )
    for chosen, source, step in choices:

        @pl.when(chosen)
        def _(source=source, step=step):
            pltpu.make_async_copy(source.at[step, 1], own, sems.at[3]).start()
            pltpu.make_async_copy(source.at[step, 0], far, sems.at[4]).start()

    for copy in copies:
        copy.wait()
    odd = parity()
    edge = halo.shape[1]
    pltpu.make_async_copy(states.at[0, 1], own, sems.at[3]).wait()
    rows = normalised(own[...], gain[...])
    normed[...] = rows
    picked = picked_rows(rows, halo, odd)
    cross[:edge], inner[...] = picked[:edge], picked[edge:]
    pltpu.make_async_copy(states.at[0, 0], far, sems.at[4]).wait()
    low, high = halo[0:1], halo[1:2]
    cross[edge:] = rows_of(normalised(far[...], gain[...]), jnp.where(odd == 1, high, low))


def queries_of(rows, weight):
    return jnp.dot(rows, weight, preferred_element_type=F32).astype(BF) * BF(HEAD_DIM ** -0.5)


def stream_body(normed, wq, wk, wv, wo, q, vq, vk, vv, vo, sems):
    copies = []
    for i, (source, target) in enumerate(((wq, vq), (wk, vk), (wv, vv), (wo, vo))):
        depth = source.shape[0] // CHUNKS
        for j in range(CHUNKS):
            at = pl.ds(j * depth, depth)
            copies.append(pltpu.make_async_copy(source.at[at], target.at[at], sems.at[i, j]))
            copies[-1].start()
    for copy in copies[:CHUNKS]:
        copy.wait()
    q[...] = queries_of(normed[...], vq[...])
    for copy in copies[CHUNKS:]:
        copy.wait()


def project_first_body(normed, wq, senders, q, table):
    bias_table(senders, parity(), table)
    q[...] = queries_of(normed[...], wq[...])


def project_pass_body(normed, wq, inner, q, passed):
    passed[...] = inner[...]
    q[...] = queries_of(normed[...], wq[...])


def project_body(normed, wq, q):
    q[...] = queries_of(normed[...], wq[...])


def far_first_body(far, gain, halo, token, normed, inner):
    rows = normalised(far[...], gain[...])
    normed[...] = rows
    low, high = halo[0:1], halo[1:2]
    inner[...] = rows_of(rows, jnp.where(parity() == 1, low, high))


def attention(q, normed, cross, inner, table, wk, wv, attended):
    rows = jnp.concatenate([normed[...], cross, inner], axis=0)
    k = jnp.dot(rows, wk[...], preferred_element_type=F32).astype(BF)
    v = jnp.dot(rows, wv[...], preferred_element_type=F32).astype(BF)
    bias = table[...]
    nodes, width = q.shape
    bias = jnp.concatenate([bias, bias], axis=0)
    first = lax.broadcasted_iota(jnp.int32, (nodes, LANES), 1) < HEAD_DIM
    ones = jnp.ones((table.shape[1], LANES), BF)
    for i in range(width // LANES):
        at = slice(i * LANES, (i + 1) * LANES)
        pair = q[:, at]
        zero = jnp.zeros_like(pair)
        both = jnp.concatenate([jnp.where(first, pair, zero), jnp.where(first, zero, pair)], axis=0)
        scores = lax.dot_general(both, k[:, at], (((1,), (1,)), ((), ())), preferred_element_type=F32) + bias
        expo = jnp.exp(scores - jnp.max(scores, axis=1, keepdims=True)).astype(BF)
        sums = jnp.dot(expo, jnp.concatenate([v[:, at], ones], axis=1), preferred_element_type=F32)
        top = sums[:nodes, :LANES] / sums[:nodes, LANES:]
        low = sums[nodes:, :LANES] / sums[nodes:, LANES:]
        attended[:, at] = jnp.where(first, top, low).astype(BF)


def attend(state, q, normed, cross, inner, table, wk, wv, wo, attended):
    attention(q, normed, cross, inner, table, wk, wv, attended)
    update = jnp.dot(attended[...], wo[...], preferred_element_type=F32)
    return (state[...].astype(F32) + update).astype(BF)


def middle_body(splits, state, q, normed, cross, inner, table, wk, wv, wo, gain, halo,
                new_state, new_normed, new_cross, new_inner, *rest):
    edge = halo.shape[1]
    if splits:
        later, attended = rest
        later[...] = cross[edge:]
    else:
        attended, = rest
    moved = attend(state, q, normed, cross[:edge], inner[...], table, wk, wv, wo, attended)
    new_state[...] = moved
    rows = normalised(moved, gain[...])
    new_normed[...] = rows
    picked = picked_rows(rows, halo, parity())
    new_cross[...] = picked[:edge]
    new_inner[...] = picked[edge:]


def last_body(index, state, q, normed, cross, inner, table, wk, wv, wo, out, attended):
    special = lax.axis_index("lead") == index

    @pl.when(special)
    def _():
        out[...] = state[...]

    @pl.when(jnp.logical_not(special))
    def _():
        out[...] = attend(state, q, normed, cross[...], inner[...], table, wk, wv, wo, attended)


def finish_body(index, state, q, normed, cross, inner, table, wk, wv, wo, arrived, out, attended, result, sems):
    there = pltpu.make_async_copy(arrived, out.at[0, 1], sems.at[0])
    there.start()
    special = lax.axis_index("lead") == index

    @pl.when(special)
    def _():
        result[...] = state[...]

    @pl.when(jnp.logical_not(special))
    def _():
        result[...] = attend(state, q, normed, cross[...], inner[...], table, wk, wv, wo, attended)

    here = pltpu.make_async_copy(result, out.at[0, 0], sems.at[1])
    here.start()
    there.wait()
    here.wait()


def per_device(states, entering, norm_gain, wq, wk, wv, wo, senders, halo_rows):
    leads, places = lax.axis_size("lead"), lax.axis_size("mesh")
    members, nodes, width = states.shape[1:]
    edge = halo_rows.shape[2]
    gain, halo, senders = norm_gain[None], halo_rows[0], senders.T
    states, entering = (pltpu.with_memory_space_constraint(x, pltpu.HBM) for x in (states, entering))
    vq, vk, vv, vo = wq, wk, wv, wo
    inner_route = [(i, i ^ 1) for i in range(places)]
    cross_route = [
        (a * places + i, ((a + leads // 2) % leads) * places + i if i in (0, places - 1) else a * places + ((i - 1) ^ 1) + 1)
        for a in range(leads)
        for i in range(places)
    ]
    route = [(i, (i + 2) % leads) for i in range(leads)]
    block, rim, rims = shape(nodes, width), shape(edge, width), shape(2 * edge, width)
    dma = pltpu.SemaphoreType.DMA

    def crossed(cross):
        return lax.ppermute(cross, ("lead", "mesh"), cross_route)

    def swapped(inner):
        return lax.ppermute(inner, "mesh", inner_route)

    def project(normed):
        return call(project_body, "project", [normed, vq], [VMEM] * 2, block, VMEM, micros=MP)

    def project_pass(normed, inner):
        return call(
            project_pass_body, "project", [normed, vq, inner], [VMEM] * 3, [block, rim], [VMEM] * 2, micros=MP,
        )

    def middle(name, splits, state, q, normed, cross, inner):
        return call(
            functools.partial(middle_body, splits), name,
            [state, q, normed, cross, inner, table, vk, vv, vo, gain, halo], [VMEM] * 11,
            [block, block, rim, rim] + [rim] * splits, [VMEM] * (4 + splits), [pltpu.VMEM((nodes, width), BF)],
        )

    def last(name, index, state, q, normed, cross, inner):
        return call(
            functools.partial(last_body, index), name,
            [state, q, normed, cross, inner, table, vk, vv, vo], [VMEM] * 9,
            block, VMEM, [pltpu.VMEM((nodes, width), BF)], micros=ML,
        )

    far, state1, gain, halo, normed1, cross, inner = call(
        functools.partial(start_body, leads - 2, leads - 1), "start",
        [states, entering] + [pltpu.with_memory_space_constraint(x, pltpu.HBM) for x in (gain, halo)],
        [HBM] * 4,
        [block, block] + [shape(*x.shape, dtype=x.dtype) for x in (gain, halo)] + [block, rims, rim],
        [VMEM] * 7, [dma((5,))], micros=MS,
    )
    cross = crossed(cross)
    inner = swapped(inner)
    q1, table = call(
        project_first_body, "project_first", [normed1, vq, senders], [VMEM] * 3,
        [block, shape(nodes, nodes + 2 * edge, dtype=F32)], [VMEM] * 2, micros=MP,
    )
    far = lax.ppermute(far, "lead", route)
    state1, normed1, cross1, inner1, halo0 = middle("middle_1", True, state1, q1, normed1, cross, inner)
    cross1 = crossed(cross1)
    inner1 = swapped(inner1)
    q1, halo0 = project_pass(normed1, halo0)
    halo0 = lax.ppermute(halo0, "lead", route)
    near = last("last_1", leads - 2, state1, q1, normed1, cross1, inner1)
    arrived = lax.ppermute(near, "lead", route)
    normed0, inner0 = call(
        far_first_body, "far_first", [far, gain, halo, near], [VMEM] * 3 + [ANY], [block, rim], [VMEM] * 2,
    )
    inner0 = swapped(inner0)
    q0 = project(normed0)
    state0, normed0, cross0, inner0 = middle("middle_0", False, far, q0, normed0, halo0, inner0)
    cross0 = crossed(cross0)
    inner0 = swapped(inner0)
    q0 = project(normed0)
    return call(
        functools.partial(finish_body, 0), "finish",
        [state0, q0, normed0, cross0, inner0, table, vk, vv, vo, arrived], [VMEM] * 10,
        shape(1, members, nodes, width), HBM,
        [pltpu.VMEM((nodes, width), BF)] * 2 + [dma((2,))],
    )


def solution(mesh):
    P = jax.sharding.PartitionSpec
    in_specs = (
        P("lead", None, "mesh", None),
        P(None, None, "mesh", None),
        P(),
        P(),
        P(),
        P(),
        P(),
        P("mesh", None),
        P("mesh", None, None),
    )
    return jax.shard_map(
        per_device, mesh=mesh, in_specs=in_specs, out_specs=P("lead", None, "mesh", None), check_vma=False
    )
```
